32 devices in a mesh: tm: 32 (over z, y, x, core), tile: 1.
Axes of the slice: x: 2, y: 2, z: 4, core: 2. Of those that a mesh axis runs over, the one named last changes fastest.
Arguments:
- movie_frames: bfloat16 [32, 1024, 1024], P('tm', None, 'tile'), may hold values from -6 to 6
- patch_weight: bfloat16 [64, 128], replicated, may hold values from -0.75 to 0.75
- depth_weight: bfloat16 [3, 3, 3, 128], replicated, may hold values from -4 to 4
- point_weight: bfloat16 [3, 128, 128], replicated, may hold values from -0.5 to 0.5
- observe_weight: bfloat16 [16, 16, 128, 256], P('tile'), may hold values from -0.03125 to 0.03125
- input_map: float32 [256, 256], replicated, may hold values from -0.375 to 0.375
- mode_decay: float32 [128], replicated, may hold values from 0.86 to 1, as said below
- mode_angle: float32 [128], replicated, may hold values from -0.1 to 0.1
- smooth_decay: float32 [128], replicated, may hold values from 0.86 to 1, as said below
- smooth_angle: float32 [128], replicated, may hold values from -0.1 to 0.1
- readout: float32 [256, 256], replicated, may hold values from -0.375 to 0.375
Outputs:
- latent: float32 [32, 256], P('tm', 'tile')
The draws below stay inside these ranges and needn't reach their ends.
Inputs may be any that keep to these rules, and one draw needn't show every extreme that they name: `mode_decay`: every mode's magnitude per frame lies strictly below one. `smooth_decay`: every mode's gain magnitude per frame lies strictly below one.
All inputs are finite; a program needn't handle non-finite values.
Results may differ from the reference program's by a relative error of at most 0.00075.
Values may be sent and summed in bfloat16 or wider, within the bound.
A program may use at most 128 MiB of HBM per device.

```python
import jax
import jax.numpy as jnp
from jax import lax

H = 1024
W = 1024
PATCH = 8
POOL = 8
CH = 128
LAYERS = 3
OBS = 256
MODES = 128
LATENT = 256
FRAMES = 32
STATE = 256


def decay_law(key, slow_share):
    kind_key, rate_key = jax.random.split(key)
    slow_mode = jax.random.uniform(kind_key, (MODES,)) < slow_share
    spread = jax.random.uniform(rate_key, (MODES,))
    slow_rate = jnp.exp(jnp.log(0.1) + spread * jnp.log(20.0)) / FRAMES
    fast_rate = jnp.exp(jnp.log(0.05) + spread * jnp.log(3.0))
    return jnp.exp(-jnp.where(slow_mode, slow_rate, fast_rate)).astype(jnp.float32)


def draw_mode_decay(key, part):
    slow_share = 0.5
    return decay_law(jax.random.fold_in(key, 11), slow_share)


def draw_smooth_decay(key, part):
    slow_share = 0.5
    return decay_law(jax.random.fold_in(key, 23), slow_share)


def block_scale(stream_key, shape, cuts, least, top_value):
    loudness, own = 1.0, jax.random.fold_in(stream_key, 6)
    for position, blocks in cuts:
        draws = jnp.exp(jax.random.uniform(jax.random.fold_in(own, position), (blocks,), jnp.float32, least / len(cuts), top_value / len(cuts)))
        loudness = loudness * jnp.repeat(draws, shape[position] // blocks).reshape([-1 if axis == position else 1 for axis in range(len(shape))])
    return loudness


def scatter_about(key, extent, scale, most, shards=(), dtype=jnp.bfloat16):
    entries = jax.random.normal(key, extent, jnp.float32) * scale
    if len(shards) > 0:
        entries = block_scale(key, extent, shards, -0.22, 0.18) * entries
    return jnp.clip(entries, min=-most, max=most).astype(dtype)


def setup_inputs(seed: int = 0) -> dict:
    arg_keys = jax.random.split(jax.random.key(seed), 12)
    movie_frames = scatter_about(arg_keys[0], (FRAMES, H, W), 1.0, 6.0, ((0, 32),))
    patch_weight = scatter_about(arg_keys[1], (PATCH * PATCH, CH), (PATCH * PATCH) ** -0.5, 0.75)
    depth_weight = scatter_about(arg_keys[2], (LAYERS, 3, 3, CH), 2 ** -0.5, 4.0)
    point_weight = scatter_about(arg_keys[3], (LAYERS, CH, CH), CH ** -0.5, 0.5)
    observe_weight = scatter_about(arg_keys[4], (W // (PATCH * POOL), H // (PATCH * POOL), CH, OBS), ((W // (PATCH * POOL)) * (H // (PATCH * POOL)) * CH) ** -0.5, 0.03125)
    input_map = scatter_about(arg_keys[5], (STATE, OBS), OBS ** -0.5, 0.375, (), jnp.float32)
    mode_decay = draw_mode_decay(jax.random.fold_in(arg_keys[11], 71), 0)
    mode_angle = jnp.clip(jax.random.uniform(arg_keys[7], (MODES,), jnp.float32, -0.1, 0.1), -0.1, 0.1)
    smooth_decay = draw_smooth_decay(jax.random.fold_in(arg_keys[11], 71), 0)
    smooth_angle = jnp.clip(jax.random.uniform(arg_keys[9], (MODES,), jnp.float32, -0.1, 0.1), -0.1, 0.1)
    readout = scatter_about(arg_keys[10], (LATENT, STATE), STATE ** -0.5, 0.375, (), jnp.float32)
    return {"movie_frames": movie_frames, "patch_weight": patch_weight, "depth_weight": depth_weight, "point_weight": point_weight, "observe_weight": observe_weight, "input_map": input_map, "mode_decay": mode_decay, "mode_angle": mode_angle, "smooth_decay": smooth_decay, "smooth_angle": smooth_angle, "readout": readout}


def encode(single_frame, patch_weight, depth_weight, point_weight):
    grid_rows = single_frame.shape[0] // PATCH
    grid_cols = single_frame.shape[1] // PATCH
    patches = single_frame.reshape(grid_rows, PATCH, grid_cols, PATCH).transpose(0, 2, 1, 3).reshape(grid_rows, grid_cols, PATCH * PATCH)
    hidden = jax.nn.gelu(jnp.dot(patches, patch_weight, preferred_element_type=jnp.float32)).astype(jnp.bfloat16)
    for layer_index in range(LAYERS):
        padded = jnp.pad(hidden, ((1, 1), (1, 1), (0, 0)))
        summed = jnp.zeros(hidden.shape, jnp.float32)
        for row_shift in range(3):
            for col_shift in range(3):
                kernel = depth_weight[layer_index, row_shift, col_shift].astype(jnp.float32)
                summed = summed + padded[row_shift:row_shift + grid_rows, col_shift:col_shift + grid_cols].astype(jnp.float32) * kernel
        depthwise = summed.astype(jnp.bfloat16)
        branch = jax.nn.gelu(jnp.dot(depthwise, point_weight[layer_index], preferred_element_type=jnp.float32))
        hidden = (hidden.astype(jnp.float32) + branch).astype(jnp.bfloat16)
    pooled = lax.optimization_barrier(jnp.mean(hidden.astype(jnp.float32).reshape(grid_rows // POOL, POOL, grid_cols // POOL, POOL, CH), axis=(1, 3))).astype(jnp.bfloat16)
    return pooled.transpose(1, 0, 2).reshape(-1)

def rotate(state, magnitude, cosine, sine):
    real_part = state[..., 0]
    imag_part = state[..., 1]
    return jnp.stack([magnitude * (cosine * real_part - sine * imag_part), magnitude * (sine * real_part + cosine * imag_part)], axis=-1)

def run_chain(inputs, magnitude, cosine, sine, initial, backward):

    def advance(state, element):
        updated = rotate(state, magnitude, cosine, sine) + element
        return (updated, updated)
    final_state, states = lax.scan(advance, initial, inputs, reverse=backward)
    return states

def reference(movie_frames, patch_weight, depth_weight, point_weight, observe_weight, input_map, mode_decay, mode_angle, smooth_decay, smooth_angle, readout):

    def encode_one(single_frame):
        return encode(single_frame, patch_weight, depth_weight, point_weight)
    features = lax.map(encode_one, movie_frames)
    observed = jnp.dot(features, observe_weight.reshape(-1, OBS), preferred_element_type=jnp.float32)
    drive = jnp.dot(observed, input_map.T, precision=lax.Precision.HIGHEST).reshape(FRAMES, MODES, 2)
    drive = drive * jnp.sqrt(1.0 - mode_decay * mode_decay)[:, None]
    zero_state = jnp.zeros((MODES, 2), jnp.float32)
    filtered = run_chain(drive, mode_decay, jnp.cos(mode_angle), jnp.sin(mode_angle), zero_state, False)
    weighted = filtered * jnp.sqrt(1.0 - smooth_decay * smooth_decay)[:, None]
    smoothed = run_chain(weighted, smooth_decay, jnp.cos(smooth_angle), jnp.sin(smooth_angle), zero_state, True)
    return jnp.dot(smoothed.reshape(FRAMES, STATE), readout.T, precision=lax.Precision.HIGHEST)
```

```python
import functools
import math

import jax
import jax.numpy as jnp
from jax import lax
from jax.experimental import pallas as pl
from jax.experimental.pallas import tpu as pltpu
from jax.sharding import PartitionSpec as P

PATCH = 8
POOL = 8
LAYERS = 3


def with_halo(x, sides, width):
    for axis, dim in sides:
        size, length = (lax.axis_size(axis), x.shape[dim])
        up = [(i, (i + 1) % size) for i in range(size - 1)]
        down = [(j, i) for i, j in up]
        last = lax.slice_in_dim(x, length - width, length, axis=dim)
        initial = lax.slice_in_dim(x, 0, width, axis=dim)
        before = lax.ppermute(last, axis, up)
        after = lax.ppermute(initial, axis, down)
        x = jnp.concatenate([before, x, after], axis=dim)
    return x


def embed(frames, patch_weight):
    frame_count, height, width = frames.shape
    grid_rows = height // PATCH
    grid_cols = width // PATCH
    patches = (
        frames.reshape(frame_count, grid_rows, PATCH, grid_cols, PATCH)
        .transpose(0, 1, 3, 2, 4)
        .reshape(frame_count, grid_rows, grid_cols, PATCH * PATCH)
    )
    return jax.nn.gelu(jnp.dot(patches, patch_weight, preferred_element_type=jnp.float32)).astype(
        jnp.bfloat16
    )


def conv_layer(hidden, padded, depth_weight, point_weight, layer_index):
    grid_rows = hidden.shape[1]
    grid_cols = hidden.shape[2]
    summed = jnp.zeros(hidden.shape, jnp.float32)
    for row_shift in range(3):
        for col_shift in range(3):
            kernel = depth_weight[layer_index, row_shift, col_shift].astype(jnp.float32)
            summed = (
                summed
                + padded[
                    :, row_shift : row_shift + grid_rows, col_shift : col_shift + grid_cols
                ].astype(jnp.float32)
                * kernel
            )
    depthwise = summed.astype(jnp.bfloat16)
    branch = jax.nn.gelu(
        jnp.dot(depthwise, point_weight[layer_index], preferred_element_type=jnp.float32)
    )
    return (hidden.astype(jnp.float32) + branch).astype(jnp.bfloat16)

GELU_LINEAR = 2.0 * math.sqrt(2.0 / math.pi)
GELU_CUBIC = 4.0 * 0.044715 * GELU_LINEAR
EDGE = 8
GROUP = 8
STRIP = 16


def gelu_of_half(half):
    inner = half * (GELU_LINEAR + GELU_CUBIC * (half * half))
    return half + half * jnp.tanh(inner)


def encoder_kernel(
    frame_ref,
    patch_ref,
    depth_ref,
    point_ref,
    observe_ref,
    out_ref,
    cells,
    spread,
    first,
    second,
    mixed,
    depth_rows,
    point_pair,
    observe,
    observe_sem,
):
    height, width = frame_ref.shape
    channels = patch_ref.shape[1]
    rows, cols = height // PATCH, width // PATCH
    lane_groups = width // 128
    group_cols = 128 // PATCH
    pool_cols, pool_rows = cols // POOL, rows // POOL

    def observe_copy(index):
        return pltpu.make_async_copy(
            observe_ref.at[index], observe.at[index], observe_sem.at[index]
        )

    for index in range(pool_cols):
        observe_copy(index).start()

    patch = patch_ref[...].astype(jnp.float32) * 0.5
    blank = jnp.zeros((PATCH, channels), jnp.float32)
    spread[...] = jnp.zeros_like(spread)
    for i in range(PATCH):
        part = patch[i * PATCH : (i + 1) * PATCH]
        block = jnp.concatenate(
            [
                jnp.concatenate([part, blank], axis=1),
                jnp.concatenate([blank, part], axis=1),
            ],
            axis=0,
        ).astype(jnp.bfloat16)
        for n in range(group_cols // 2):
            spread[n, pl.ds(i * 128 + n * 2 * PATCH, 2 * PATCH), :] = block
    square = jnp.zeros((channels, channels), jnp.bfloat16)
    for layer in range(LAYERS):
        point = (point_ref[layer].astype(jnp.float32) * 0.5).astype(jnp.bfloat16)
        point_pair[layer, :channels, :channels] = point
        point_pair[layer, channels:, channels:] = point
        point_pair[layer, :channels, channels:] = square
        point_pair[layer, channels:, :channels] = square
    depth = depth_ref[...].astype(jnp.float32)
    for tap in range(LAYERS * 9):
        depth_rows[tap] = jnp.broadcast_to(depth[tap : tap + 1], (STRIP, channels))

    for ref in (first, second):
        column = jnp.zeros(ref.shape[1:], jnp.float32)
        ref[0] = column
        ref[cols + 1] = column
        edge = jnp.zeros((cols + 2, EDGE, channels), jnp.float32)
        ref[:, :EDGE, :] = edge
        ref[:, EDGE + rows :, :] = edge

    row_block = 256
    row_cells = row_block // PATCH
    to_row = lax.broadcasted_iota(jnp.int32, (row_block, row_block), 0)
    from_row = lax.broadcasted_iota(jnp.int32, (row_block, row_block), 1)
    order = jnp.where(
        (from_row % PATCH == to_row // row_cells) & (from_row // PATCH == to_row % row_cells),
        1.0,
        0.0,
    ).astype(jnp.bfloat16)
    for b in range(height // row_block):
        ordered = jnp.dot(
            order,
            frame_ref[b * row_block : (b + 1) * row_block, :],
            preferred_element_type=jnp.float32,
        ).astype(jnp.bfloat16)
        for g in range(lane_groups):
            for i in range(PATCH):
                cells[
                    g, b * row_cells : (b + 1) * row_cells, i * 128 : (i + 1) * 128
                ] = ordered[i * row_cells : (i + 1) * row_cells, g * 128 : (g + 1) * 128]

    half_groups = max(lane_groups // 2, 1)

    def embed_step(step, carry):
        n = step // (lane_groups // half_groups)
        part = step % (lane_groups // half_groups)
        taken = cells[pl.ds(part * half_groups, half_groups)].reshape(
            half_groups * rows, PATCH * 128
        )
        half = jnp.dot(taken, spread[n], preferred_element_type=jnp.float32)
        for g in range(half_groups):
            value = gelu_of_half(half[g * rows : (g + 1) * rows])
            value = value.astype(jnp.bfloat16).astype(jnp.float32)
            column = (part * half_groups + g) * group_cols + 2 * n + 1
            first[column, EDGE : EDGE + rows, :] = value[:, :channels]
            first[column + 1, EDGE : EDGE + rows, :] = value[:, channels:]
        return carry

    lax.fori_loop(0, (group_cols // 2) * (lane_groups // half_groups), embed_step, 0)

    def layer_branch(layer, source, group):
        start = group * GROUP
        for p in range(GROUP // 2):
            for strip in range(rows // STRIP):
                sums = [None, None]
                for dr in range(3):
                    for cc in range(4):
                        taken = source[
                            start + 2 * p + cc, pl.ds(EDGE - 1 + strip * STRIP + dr, STRIP), :
                        ]
                        for o in range(2):
                            dc = cc - o
                            if 0 <= dc <= 2:
                                term = taken * depth_rows[layer * 9 + dr * 3 + dc]
                                sums[o] = term if sums[o] is None else sums[o] + term
                for o in range(2):
                    mixed[
                        p * rows + strip * STRIP : p * rows + (strip + 1) * STRIP,
                        o * channels : (o + 1) * channels,
                    ] = sums[o].astype(jnp.bfloat16)
        return jnp.dot(mixed[...], point_pair[layer], preferred_element_type=jnp.float32)

    def updated(source, group, half, p, o):
        column = group * GROUP + 2 * p + o + 1
        branch = gelu_of_half(
            half[p * rows : (p + 1) * rows, o * channels : (o + 1) * channels]
        )
        value = source[column, EDGE : EDGE + rows, :] + branch
        return column, value.astype(jnp.bfloat16).astype(jnp.float32)

    def layer_step(layer, source, target, group, carry):
        half = layer_branch(layer, source, group)
        for p in range(GROUP // 2):
            for o in range(2):
                column, value = updated(source, group, half, p, o)
                target[column, EDGE : EDGE + rows, :] = value
        return carry

    def last_step(source, group, total):
        half = layer_branch(LAYERS - 1, source, group)
        summed = jnp.zeros((rows, channels), jnp.float32)
        for p in range(GROUP // 2):
            for o in range(2):
                summed = summed + updated(source, group, half, p, o)[1]
        pooled = jnp.sum(summed.reshape(pool_rows, POOL, channels), axis=1) * (
            1.0 / (POOL * POOL)
        )
        own = lax.broadcasted_iota(jnp.int32, (pool_rows, channels), 0)
        features = jnp.concatenate(
            [jnp.where(own == r, pooled, 0.0) for r in range(pool_rows)], axis=1
        ).astype(jnp.bfloat16)
        observe_copy(group).wait()
        return total + jnp.dot(features, observe[group], preferred_element_type=jnp.float32)

    refs = (first, second)
    for layer in range(LAYERS - 1):
        lax.fori_loop(
            0,
            cols // GROUP,
            functools.partial(layer_step, layer, refs[layer % 2], refs[(layer + 1) % 2]),
            0,
        )
    total = lax.fori_loop(
        0,
        pool_cols,
        functools.partial(last_step, refs[(LAYERS - 1) % 2]),
        jnp.zeros((pool_rows, observe.shape[2]), jnp.float32),
    )
    out_ref[...] = jnp.sum(total, axis=0, keepdims=True)


def encode_whole(frame, patch_weight, depth_weight, point_weight, observe_weight):
    height, width = frame.shape
    channels = patch_weight.shape[1]
    rows, cols = height // PATCH, width // PATCH
    pool_cols, pool_rows, _, components = observe_weight.shape
    observe_weight = observe_weight.reshape(pool_cols, pool_rows * channels, components)
    vmem = pl.BlockSpec(memory_space=pltpu.VMEM)
    padded = (cols + 2, rows + 2 * EDGE, channels)
    return pl.pallas_call(
        encoder_kernel,
        out_shape=jax.ShapeDtypeStruct((1, components), jnp.float32),
        in_specs=[vmem, vmem, vmem, vmem, pl.BlockSpec(memory_space=pl.ANY)],
        out_specs=vmem,
        scratch_shapes=[
            pltpu.VMEM((width // 128, rows, PATCH * 128), jnp.bfloat16),
            pltpu.VMEM((128 // PATCH // 2, PATCH * 128, 2 * channels), jnp.bfloat16),
            pltpu.VMEM(padded, jnp.float32),
            pltpu.VMEM(padded, jnp.float32),
            pltpu.VMEM((GROUP // 2 * rows, 2 * channels), jnp.bfloat16),
            pltpu.VMEM((LAYERS * 9, STRIP, channels), jnp.float32),
            pltpu.VMEM((LAYERS, 2 * channels, 2 * channels), jnp.bfloat16),
            pltpu.VMEM(observe_weight.shape, jnp.bfloat16),
            pltpu.SemaphoreType.DMA((pool_cols,)),
        ],
        compiler_params=pltpu.CompilerParams(vmem_limit_bytes=60 * 1024 * 1024),
        name="encoder",
    )(frame, patch_weight, depth_weight.reshape(-1, channels), point_weight, observe_weight)


def complex_times(a, b):
    return (a[0] * b[0] - a[1] * b[1], a[0] * b[1] + a[1] * b[0])


def filter_kernel(
    count, observed_ref, map_ref, modes_ref, readout_ref, out_ref, gathered, send_sem, recv_sem
):
    me = lax.axis_index("tm")
    barrier = pltpu.get_barrier_semaphore()

    def greet(step, carry):
        pl.semaphore_signal(
            barrier,
            inc=1,
            device_id={"tm": lax.rem(me + step, count)},
            device_id_type=pl.DeviceIdType.MESH,
        )
        return carry

    lax.fori_loop(1, count, greet, 0)

    modes = modes_ref.shape[1]
    state = 2 * modes
    mode = lax.broadcasted_iota(jnp.int32, (modes, state), 0)
    component = lax.broadcasted_iota(jnp.int32, (modes, state), 1)
    repeat = jnp.where(component // 2 == mode, 1.0, 0.0)
    doubled = jnp.dot(
        modes_ref[...],
        repeat,
        precision=lax.Precision.HIGHEST,
        preferred_element_type=jnp.float32,
    )
    decay, angle, back_decay, back_angle = (doubled[k : k + 1] for k in range(4))
    drive = lax.dot_general(
        observed_ref[...],
        map_ref[...],
        (((1,), (1,)), ((), ())),
        precision=lax.Precision.HIGHEST,
        preferred_element_type=jnp.float32,
    ) * jnp.sqrt(1.0 - decay * decay)
    gathered[pl.ds(me, 1)] = drive.reshape(1, 1, state)
    pl.semaphore_wait(barrier, count - 1)

    def copy_to(step):
        return pltpu.make_async_remote_copy(
            src_ref=gathered.at[me],
            dst_ref=gathered.at[me],
            send_sem=send_sem.at[step],
            recv_sem=recv_sem.at[me],
            device_id={"tm": lax.rem(me + step, count)},
            device_id_type=pl.DeviceIdType.MESH,
        )

    def send(step, carry):
        copy_to(step).start()
        return carry

    lax.fori_loop(1, count, send, 0)

    forward = (decay * jnp.cos(angle), decay * jnp.sin(angle))
    backward = (back_decay * jnp.cos(back_angle), back_decay * jnp.sin(back_angle))
    both = complex_times(forward, backward)
    frame = lax.broadcasted_iota(jnp.int32, (count, state), 0)
    one = (jnp.ones((1, state), jnp.float32), jnp.zeros((1, state), jnp.float32))
    power, partial = one, one
    partial_sums = [one]
    for _ in range(count - 1):
        power = complex_times(power, both)
        partial = (partial[0] + power[0], partial[1] + power[1])
        partial_sums.append(partial)
    last = jnp.maximum(frame, me)
    sums = [jnp.zeros((count, state), jnp.float32) for _ in range(2)]
    for n in range(count):
        for k in range(2):
            sums[k] = jnp.where(last == count - 1 - n, partial_sums[n][k], sums[k])
    away = jnp.abs(frame - me)
    factor = tuple(jnp.where(frame > me, backward[k], forward[k]) for k in range(2))
    gain = tuple(sums)
    bit = 1
    while bit < count:
        taken = complex_times(gain, factor)
        chosen = (away // bit) % 2 == 1
        gain = tuple(jnp.where(chosen, taken[k], gain[k]) for k in range(2))
        factor = complex_times(factor, factor)
        bit = bit * 2
    weight = jnp.sqrt(1.0 - back_decay * back_decay)
    imaginary = lax.broadcasted_iota(jnp.int32, (count, state), 1) % 2 == 1
    direct = gain[0] * weight
    crossed = jnp.where(imaginary, gain[1], -gain[1]) * weight

    def arrive(step, carry):
        source = lax.rem(me + step, count)
        pltpu.make_async_remote_copy(
            src_ref=gathered.at[source],
            dst_ref=gathered.at[source],
            send_sem=send_sem.at[step],
            recv_sem=recv_sem.at[source],
            device_id={"tm": source},
            device_id_type=pl.DeviceIdType.MESH,
        ).wait_recv()
        return carry

    lax.fori_loop(1, count, arrive, 0)
    drives = gathered[...].reshape(count, state)
    partner = jnp.where(
        imaginary, pltpu.roll(drives, 1, 1), pltpu.roll(drives, state - 1, 1)
    )
    smoothed = jnp.sum(direct * drives + crossed * partner, axis=0, keepdims=True)
    out_ref[...] = lax.dot_general(
        smoothed,
        readout_ref[...],
        (((1,), (1,)), ((), ())),
        precision=lax.Precision.HIGHEST,
        preferred_element_type=jnp.float32,
    )

    def sent(step, carry):
        copy_to(step).wait_send()
        return carry

    lax.fori_loop(1, count, sent, 0)


def filtered_latent(observed, input_map, modes, readout):
    count = lax.axis_size("tm")
    state = observed.shape[1]
    vmem = pl.BlockSpec(memory_space=pltpu.VMEM)
    return pl.pallas_call(
        functools.partial(filter_kernel, count),
        out_shape=jax.ShapeDtypeStruct((1, readout.shape[0]), jnp.float32),
        in_specs=[vmem] * 4,
        out_specs=vmem,
        scratch_shapes=[
            pltpu.VMEM((count, 1, state), jnp.float32),
            pltpu.SemaphoreType.DMA((count,)),
            pltpu.SemaphoreType.DMA((count,)),
        ],
        compiler_params=pltpu.CompilerParams(collective_id=0, has_side_effects=True),
        name="filters",
    )(observed, input_map, modes, readout)


def encode_tiles(frames, patch_weight, depth_weight, point_weight, observe_weight):
    frame_count, height, width = frames.shape
    grid_rows = height // PATCH
    grid_cols = width // PATCH
    channels = patch_weight.shape[1]
    hidden = embed(frames, patch_weight)
    for layer_index in range(LAYERS):
        widened = with_halo(hidden, (("tile", 2),), 1)
        padded = jnp.pad(widened, ((0, 0), (1, 1), (0, 0), (0, 0)))
        hidden = conv_layer(hidden, padded, depth_weight, point_weight, layer_index)
    pooled = jnp.mean(
        hidden.astype(jnp.float32).reshape(
            frame_count, grid_rows // POOL, POOL, grid_cols // POOL, POOL, channels
        ),
        axis=(2, 4),
    ).astype(jnp.bfloat16)
    features = pooled.transpose(0, 2, 1, 3).reshape(frame_count, -1)
    partial_value = jnp.dot(
        features,
        observe_weight.reshape(-1, observe_weight.shape[-1]),
        preferred_element_type=jnp.float32,
    )
    return lax.psum(partial_value, "tile")


def shards(
    movie_frames,
    patch_weight,
    depth_weight,
    point_weight,
    observe_weight,
    input_map,
    mode_decay,
    mode_angle,
    smooth_decay,
    smooth_angle,
    readout,
):
    tile_count = lax.axis_size("tile")
    encoder = (patch_weight, depth_weight, point_weight, observe_weight)
    if tile_count == 1:
        observed = encode_whole(movie_frames[0], *encoder)
    else:
        observed = encode_tiles(movie_frames, *encoder)
        share = readout.shape[0] // tile_count
        readout = lax.dynamic_slice_in_dim(readout, lax.axis_index("tile") * share, share, 0)
    modes = jnp.stack([mode_decay, mode_angle, smooth_decay, smooth_angle])
    return filtered_latent(observed, input_map, modes, readout)


def solution(mesh):
    placed = (
        P("tm", None, "tile"),
        P(),
        P(),
        P(),
        P("tile", None, None, None),
        P(),
        P(),
        P(),
        P(),
        P(),
        P(),
    )
    return jax.shard_map(
        shards, mesh=mesh, in_specs=placed, out_specs=P("tm", "tile"), check_vma=False
    )
```

```python
import functools
import math

import jax
import jax.numpy as jnp
from jax import lax
from jax.experimental import pallas as pl
from jax.experimental.pallas import tpu as pltpu
from jax.sharding import PartitionSpec as P

PATCH = 8
POOL = 8
LAYERS = 3


def with_halo(x, sides, width):
    for axis, dim in sides:
        size, length = (lax.axis_size(axis), x.shape[dim])
        up = [(i, (i + 1) % size) for i in range(size - 1)]
        down = [(j, i) for i, j in up]
        last = lax.slice_in_dim(x, length - width, length, axis=dim)
        initial = lax.slice_in_dim(x, 0, width, axis=dim)
        before = lax.ppermute(last, axis, up)
        after = lax.ppermute(initial, axis, down)
        x = jnp.concatenate([before, x, after], axis=dim)
    return x


def embed(frames, patch_weight):
    frame_count, height, width = frames.shape
    grid_rows = height // PATCH
    grid_cols = width // PATCH
    patches = (
        frames.reshape(frame_count, grid_rows, PATCH, grid_cols, PATCH)
        .transpose(0, 1, 3, 2, 4)
        .reshape(frame_count, grid_rows, grid_cols, PATCH * PATCH)
    )
    return jax.nn.gelu(jnp.dot(patches, patch_weight, preferred_element_type=jnp.float32)).astype(
        jnp.bfloat16
    )


def conv_layer(hidden, padded, depth_weight, point_weight, layer_index):
    grid_rows = hidden.shape[1]
    grid_cols = hidden.shape[2]
    summed = jnp.zeros(hidden.shape, jnp.float32)
    for row_shift in range(3):
        for col_shift in range(3):
            kernel = depth_weight[layer_index, row_shift, col_shift].astype(jnp.float32)
            summed = (
                summed
                + padded[
                    :, row_shift : row_shift + grid_rows, col_shift : col_shift + grid_cols
                ].astype(jnp.float32)
                * kernel
            )
    depthwise = summed.astype(jnp.bfloat16)
    branch = jax.nn.gelu(
        jnp.dot(depthwise, point_weight[layer_index], preferred_element_type=jnp.float32)
    )
    return (hidden.astype(jnp.float32) + branch).astype(jnp.bfloat16)

GELU_LINEAR = 2.0 * math.sqrt(2.0 / math.pi)
GELU_CUBIC = 4.0 * 0.044715 * GELU_LINEAR
EDGE = 8
GROUP = 8
STRIP = 16


def gelu_of_half(half):
    inner = half * (GELU_LINEAR + GELU_CUBIC * (half * half))
    return half + half * jnp.tanh(inner)


def encoder_kernel(
    frame_ref,
    patch_ref,
    depth_ref,
    point_ref,
    observe_ref,
    out_ref,
    frame,
    cells,
    spread,
    first,
    second,
    mixed,
    depth_rows,
    point_pair,
    observe,
    frame_sem,
    observe_sem,
):
    height, width = frame_ref.shape
    channels = patch_ref.shape[1]
    rows, cols = height // PATCH, width // PATCH
    lane_groups = width // 128
    group_cols = 128 // PATCH
    pool_cols, pool_rows = cols // POOL, rows // POOL

    def observe_copy(index):
        return pltpu.make_async_copy(
            observe_ref.at[index], observe.at[index], observe_sem.at[index]
        )

    row_block = 256

    def frame_copy(index):
        taken = pl.ds(index * row_block, row_block)
        return pltpu.make_async_copy(frame_ref.at[taken], frame.at[taken], frame_sem.at[index])

    for index in range(height // row_block):
        frame_copy(index).start()
    for index in range(pool_cols):
        observe_copy(index).start()

    patch = patch_ref[...].astype(jnp.float32) * 0.5
    blank = jnp.zeros((PATCH, channels), jnp.float32)
    spread[...] = jnp.zeros_like(spread)
    for i in range(PATCH):
        part = patch[i * PATCH : (i + 1) * PATCH]
        block = jnp.concatenate(
            [
                jnp.concatenate([part, blank], axis=1),
                jnp.concatenate([blank, part], axis=1),
            ],
            axis=0,
        ).astype(jnp.bfloat16)
        for n in range(group_cols // 2):
            spread[n, pl.ds(i * 128 + n * 2 * PATCH, 2 * PATCH), :] = block
    square = jnp.zeros((channels, channels), jnp.bfloat16)
    for layer in range(LAYERS):
        point = (point_ref[layer].astype(jnp.float32) * 0.5).astype(jnp.bfloat16)
        point_pair[layer, :channels, :channels] = point
        point_pair[layer, channels:, channels:] = point
        point_pair[layer, :channels, channels:] = square
        point_pair[layer, channels:, :channels] = square
    for layer in range(LAYERS):
        for dr in range(3):
            taps = depth_ref[layer, dr].astype(jnp.float32)
            for dc in range(3):
                depth_rows[(layer * 3 + dr) * 3 + dc] = jnp.broadcast_to(
                    taps[dc : dc + 1], (8, channels)
                )

    for ref in (first, second):
        column = jnp.zeros(ref.shape[1:], jnp.float32)
        ref[0] = column
        ref[cols + 1] = column
        edge = jnp.zeros((cols + 2, EDGE, channels), jnp.float32)
        ref[:, :EDGE, :] = edge
        ref[:, EDGE + rows :, :] = edge

    row_cells = row_block // PATCH
    to_row = lax.broadcasted_iota(jnp.int32, (row_block, row_block), 0)
    from_row = lax.broadcasted_iota(jnp.int32, (row_block, row_block), 1)
    order = jnp.where(
        (from_row % PATCH == to_row // row_cells) & (from_row // PATCH == to_row % row_cells),
        1.0,
        0.0,
    ).astype(jnp.bfloat16)
    for b in range(height // row_block):
        frame_copy(b).wait()
        ordered = jnp.dot(
            order,
            frame[b * row_block : (b + 1) * row_block, :],
            preferred_element_type=jnp.float32,
        ).astype(jnp.bfloat16)
        for g in range(lane_groups):
            for i in range(PATCH):
                cells[
                    g, b * row_cells : (b + 1) * row_cells, i * 128 : (i + 1) * 128
                ] = ordered[i * row_cells : (i + 1) * row_cells, g * 128 : (g + 1) * 128]

    half_groups = max(lane_groups // 2, 1)

    def embed_step(step, carry):
        n = step // (lane_groups // half_groups)
        part = step % (lane_groups // half_groups)
        taken = cells[pl.ds(part * half_groups, half_groups)].reshape(
            half_groups * rows, PATCH * 128
        )
        half = jnp.dot(taken, spread[n], preferred_element_type=jnp.float32)
        for g in range(half_groups):
            value = gelu_of_half(half[g * rows : (g + 1) * rows])
            column = (part * half_groups + g) * group_cols + 2 * n + 1
            first[column, EDGE : EDGE + rows, :] = value[:, :channels]
            first[column + 1, EDGE : EDGE + rows, :] = value[:, channels:]
        return carry

    lax.fori_loop(0, (group_cols // 2) * (lane_groups // half_groups), embed_step, 0)

    def mix_cells(layer, source, group):
        start = group * GROUP
        weights = []
        for tap in range(9):
            one_tile = depth_rows[layer * 9 + tap]
            weights.append(jnp.concatenate([one_tile] * (STRIP // 8), axis=0))
        for strip in range(rows // STRIP):
            sums = [None] * GROUP
            for cc in range(GROUP + 2):
                for dr in range(3):
                    taken = source[start + cc, pl.ds(EDGE - 1 + strip * STRIP + dr, STRIP), :]
                    for dc in range(3):
                        o = cc - dc
                        if 0 <= o < GROUP:
                            term = taken * weights[dr * 3 + dc]
                            sums[o] = term if sums[o] is None else sums[o] + term
                if cc >= 2:
                    o = cc - 2
                    at = (o // 2) * rows + strip * STRIP
                    mixed[at : at + STRIP, (o % 2) * channels : (o % 2 + 1) * channels] = sums[
                        o
                    ].astype(jnp.bfloat16)

    def mix_channels(layer):
        return jnp.dot(mixed[...], point_pair[layer], preferred_element_type=jnp.float32)

    def updated(source, group, half, o):
        p = o // 2
        branch = gelu_of_half(
            half[p * rows : (p + 1) * rows, (o % 2) * channels : (o % 2 + 1) * channels]
        )
        return source[group * GROUP + o + 1, EDGE : EDGE + rows, :] + branch

    def finish(target, source, group, half, carry):
        for o in range(GROUP):
            target[group * GROUP + o + 1, EDGE : EDGE + rows, :] = updated(source, group, half, o)
        return carry

    def finish_pooled(source, group, half, total):
        summed = jnp.zeros((rows, channels), jnp.float32)
        for o in range(GROUP):
            summed = summed + updated(source, group, half, o)
        pooled = jnp.sum(summed.reshape(pool_rows, POOL, channels), axis=1) * (
            1.0 / (POOL * POOL)
        )
        own = lax.broadcasted_iota(jnp.int32, (pool_rows, channels), 0)
        features = jnp.concatenate(
            [jnp.where(own == r, pooled, 0.0) for r in range(pool_rows)], axis=1
        ).astype(jnp.bfloat16)
        observe_copy(group).wait()
        return total + jnp.dot(features, observe[group], preferred_element_type=jnp.float32)

    def run_layer(layer, source, finish, carry):
        groups = cols // GROUP
        mix_cells(layer, source, 0)

        def step(group, carry):
            half = mix_channels(layer)
            mix_cells(layer, source, group)
            return finish(source, group - 1, half, carry)

        carry = lax.fori_loop(1, groups, step, carry)
        return finish(source, groups - 1, mix_channels(layer), carry)

    refs = (first, second)
    for layer in range(LAYERS - 1):
        run_layer(
            layer, refs[layer % 2], functools.partial(finish, refs[(layer + 1) % 2]), 0
        )
    total = run_layer(
        LAYERS - 1,
        refs[(LAYERS - 1) % 2],
        finish_pooled,
        jnp.zeros((pool_rows, observe.shape[2]), jnp.float32),
    )
    out_ref[...] = jnp.sum(total, axis=0, keepdims=True)


def encode_whole(frame, patch_weight, depth_weight, point_weight, observe_weight):
    height, width = frame.shape
    channels = patch_weight.shape[1]
    rows, cols = height // PATCH, width // PATCH
    pool_cols, pool_rows, _, components = observe_weight.shape
    observe_weight = observe_weight.reshape(pool_cols, pool_rows * channels, components)
    vmem = pl.BlockSpec(memory_space=pltpu.VMEM)
    anywhere = pl.BlockSpec(memory_space=pl.ANY)
    padded = (cols + 2, rows + 2 * EDGE, channels)
    return pl.pallas_call(
        encoder_kernel,
        out_shape=jax.ShapeDtypeStruct((1, components), jnp.float32),
        in_specs=[anywhere, vmem, vmem, vmem, anywhere],
        out_specs=vmem,
        scratch_shapes=[
            pltpu.VMEM((height, width), jnp.bfloat16),
            pltpu.VMEM((width // 128, rows, PATCH * 128), jnp.bfloat16),
            pltpu.VMEM((128 // PATCH // 2, PATCH * 128, 2 * channels), jnp.bfloat16),
            pltpu.VMEM(padded, jnp.float32),
            pltpu.VMEM(padded, jnp.float32),
            pltpu.VMEM((GROUP // 2 * rows, 2 * channels), jnp.bfloat16),
            pltpu.VMEM((LAYERS * 9, 8, channels), jnp.float32),
            pltpu.VMEM((LAYERS, 2 * channels, 2 * channels), jnp.bfloat16),
            pltpu.VMEM(observe_weight.shape, jnp.bfloat16),
            pltpu.SemaphoreType.DMA((height // 256,)),
            pltpu.SemaphoreType.DMA((pool_cols,)),
        ],
        compiler_params=pltpu.CompilerParams(vmem_limit_bytes=60 * 1024 * 1024),
        name="encoder",
    )(frame, patch_weight, depth_weight, point_weight, observe_weight)


def complex_times(a, b):
    return (a[0] * b[0] - a[1] * b[1], a[0] * b[1] + a[1] * b[0])


def filter_kernel(
    count,
    observed_ref,
    map_ref,
    decay_ref,
    angle_ref,
    back_decay_ref,
    back_angle_ref,
    out_ref,
    gathered,
    send_sem,
    recv_sem,
):
    me = lax.axis_index("tm")
    barrier = pltpu.get_barrier_semaphore()

    def greet(step, carry):
        pl.semaphore_signal(
            barrier,
            inc=1,
            device_id={"tm": lax.rem(me + step, count)},
            device_id_type=pl.DeviceIdType.MESH,
        )
        return carry

    lax.fori_loop(1, count, greet, 0)

    mode_refs = (decay_ref, angle_ref, back_decay_ref, back_angle_ref)
    modes = decay_ref.shape[1]
    state = 2 * modes
    mode = lax.broadcasted_iota(jnp.int32, (modes, state), 0)
    component = lax.broadcasted_iota(jnp.int32, (modes, state), 1)
    repeat = jnp.where(component // 2 == mode, 1.0, 0.0)
    doubled = jnp.dot(
        jnp.concatenate([ref[...] for ref in mode_refs], axis=0),
        repeat,
        precision=lax.Precision.HIGHEST,
        preferred_element_type=jnp.float32,
    )
    decay, angle, back_decay, back_angle = (doubled[k : k + 1] for k in range(4))
    drive = lax.dot_general(
        observed_ref[...],
        map_ref[...],
        (((1,), (1,)), ((), ())),
        precision=lax.Precision.HIGHEST,
        preferred_element_type=jnp.float32,
    ) * jnp.sqrt(1.0 - decay * decay)
    gathered[pl.ds(me, 1)] = drive.reshape(1, 1, state)
    pl.semaphore_wait(barrier, count - 1)

    def copy_to(step):
        return pltpu.make_async_remote_copy(
            src_ref=gathered.at[me],
            dst_ref=gathered.at[me],
            send_sem=send_sem.at[step],
            recv_sem=recv_sem.at[me],
            device_id={"tm": lax.rem(me + step, count)},
            device_id_type=pl.DeviceIdType.MESH,
        )

    def send(step, carry):
        copy_to(step).start()
        return carry

    lax.fori_loop(1, count, send, 0)

    forward = (decay * jnp.cos(angle), decay * jnp.sin(angle))
    backward = (back_decay * jnp.cos(back_angle), back_decay * jnp.sin(back_angle))
    both = complex_times(forward, backward)
    frame = lax.broadcasted_iota(jnp.int32, (count, state), 0)
    one = (jnp.ones((1, state), jnp.float32), jnp.zeros((1, state), jnp.float32))
    power, partial = one, one
    partial_sums = [one]
    for _ in range(count - 1):
        power = complex_times(power, both)
        partial = (partial[0] + power[0], partial[1] + power[1])
        partial_sums.append(partial)
    last = jnp.maximum(frame, me)
    sums = [jnp.zeros((count, state), jnp.float32) for _ in range(2)]
    for n in range(count):
        for k in range(2):
            sums[k] = jnp.where(last == count - 1 - n, partial_sums[n][k], sums[k])
    away = jnp.abs(frame - me)
    factor = tuple(jnp.where(frame > me, backward[k], forward[k]) for k in range(2))
    gain = tuple(sums)
    bit = 1
    while bit < count:
        taken = complex_times(gain, factor)
        chosen = (away // bit) % 2 == 1
        gain = tuple(jnp.where(chosen, taken[k], gain[k]) for k in range(2))
        factor = complex_times(factor, factor)
        bit = bit * 2
    weight = jnp.sqrt(1.0 - back_decay * back_decay)
    imaginary = lax.broadcasted_iota(jnp.int32, (count, state), 1) % 2 == 1
    direct = gain[0] * weight
    crossed = jnp.where(imaginary, gain[1], -gain[1]) * weight

    def arrive(step, carry):
        source = lax.rem(me + step, count)
        pltpu.make_async_remote_copy(
            src_ref=gathered.at[source],
            dst_ref=gathered.at[source],
            send_sem=send_sem.at[step],
            recv_sem=recv_sem.at[source],
            device_id={"tm": source},
            device_id_type=pl.DeviceIdType.MESH,
        ).wait_recv()
        return carry

    lax.fori_loop(1, count, arrive, 0)
    drives = gathered[...].reshape(count, state)
    partner = jnp.where(
        imaginary, pltpu.roll(drives, 1, 1), pltpu.roll(drives, state - 1, 1)
    )
    out_ref[...] = jnp.sum(direct * drives + crossed * partner, axis=0, keepdims=True)

    def sent(step, carry):
        copy_to(step).wait_send()
        return carry

    lax.fori_loop(1, count, sent, 0)


def smoothed_state(observed, input_map, *modes):
    count = lax.axis_size("tm")
    state = input_map.shape[0]
    vmem = pl.BlockSpec(memory_space=pltpu.VMEM)
    return pl.pallas_call(
        functools.partial(filter_kernel, count),
        out_shape=jax.ShapeDtypeStruct((1, state), jnp.float32),
        in_specs=[vmem] * 6,
        out_specs=vmem,
        scratch_shapes=[
            pltpu.VMEM((count, 1, state), jnp.float32),
            pltpu.SemaphoreType.DMA((count,)),
            pltpu.SemaphoreType.DMA((count,)),
        ],
        compiler_params=pltpu.CompilerParams(collective_id=0, has_side_effects=True),
        name="filters",
    )(observed, input_map, *(mode.reshape(1, -1) for mode in modes))


def encode_tiles(frames, patch_weight, depth_weight, point_weight, observe_weight):
    frame_count, height, width = frames.shape
    grid_rows = height // PATCH
    grid_cols = width // PATCH
    channels = patch_weight.shape[1]
    hidden = embed(frames, patch_weight)
    for layer_index in range(LAYERS):
        widened = with_halo(hidden, (("tile", 2),), 1)
        padded = jnp.pad(widened, ((0, 0), (1, 1), (0, 0), (0, 0)))
        hidden = conv_layer(hidden, padded, depth_weight, point_weight, layer_index)
    pooled = jnp.mean(
        hidden.astype(jnp.float32).reshape(
            frame_count, grid_rows // POOL, POOL, grid_cols // POOL, POOL, channels
        ),
        axis=(2, 4),
    ).astype(jnp.bfloat16)
    features = pooled.transpose(0, 2, 1, 3).reshape(frame_count, -1)
    partial_value = jnp.dot(
        features,
        observe_weight.reshape(-1, observe_weight.shape[-1]),
        preferred_element_type=jnp.float32,
    )
    return lax.psum(partial_value, "tile")


def shards(
    movie_frames,
    patch_weight,
    depth_weight,
    point_weight,
    observe_weight,
    input_map,
    mode_decay,
    mode_angle,
    smooth_decay,
    smooth_angle,
    readout,
):
    tile_count = lax.axis_size("tile")
    encoder = (patch_weight, depth_weight, point_weight, observe_weight)
    if tile_count == 1:
        observed = encode_whole(movie_frames[0], *encoder)
    else:
        observed = encode_tiles(movie_frames, *encoder)
        share = readout.shape[0] // tile_count
        readout = lax.dynamic_slice_in_dim(readout, lax.axis_index("tile") * share, share, 0)
    smoothed = smoothed_state(
        observed, input_map, mode_decay, mode_angle, smooth_decay, smooth_angle
    )
    return jnp.dot(smoothed, readout.T, precision=lax.Precision.HIGHEST)


def solution(mesh):
    placed = (
        P("tm", None, "tile"),
        P(),
        P(),
        P(),
        P("tile", None, None, None),
        P(),
        P(),
        P(),
        P(),
        P(),
        P(),
    )
    return jax.shard_map(
        shards, mesh=mesh, in_specs=placed, out_specs=P("tm", "tile"), check_vma=False
    )
```

```python
import functools
import math

import jax
import jax.numpy as jnp
from jax import lax
from jax.experimental import pallas as pl
from jax.experimental.pallas import tpu as pltpu
from jax.sharding import PartitionSpec as P

PATCH = 8
POOL = 8
LAYERS = 3


def with_halo(x, sides, width):
    for axis, dim in sides:
        size, length = (lax.axis_size(axis), x.shape[dim])
        up = [(i, (i + 1) % size) for i in range(size - 1)]
        down = [(j, i) for i, j in up]
        last = lax.slice_in_dim(x, length - width, length, axis=dim)
        initial = lax.slice_in_dim(x, 0, width, axis=dim)
        before = lax.ppermute(last, axis, up)
        after = lax.ppermute(initial, axis, down)
        x = jnp.concatenate([before, x, after], axis=dim)
    return x


def embed(frames, patch_weight):
    frame_count, height, width = frames.shape
    grid_rows = height // PATCH
    grid_cols = width // PATCH
    patches = (
        frames.reshape(frame_count, grid_rows, PATCH, grid_cols, PATCH)
        .transpose(0, 1, 3, 2, 4)
        .reshape(frame_count, grid_rows, grid_cols, PATCH * PATCH)
    )
    return jax.nn.gelu(jnp.dot(patches, patch_weight, preferred_element_type=jnp.float32)).astype(
        jnp.bfloat16
    )


def conv_layer(hidden, padded, depth_weight, point_weight, layer_index):
    grid_rows = hidden.shape[1]
    grid_cols = hidden.shape[2]
    summed = jnp.zeros(hidden.shape, jnp.float32)
    for row_shift in range(3):
        for col_shift in range(3):
            kernel = depth_weight[layer_index, row_shift, col_shift].astype(jnp.float32)
            summed = (
                summed
                + padded[
                    :, row_shift : row_shift + grid_rows, col_shift : col_shift + grid_cols
                ].astype(jnp.float32)
                * kernel
            )
    depthwise = summed.astype(jnp.bfloat16)
    branch = jax.nn.gelu(
        jnp.dot(depthwise, point_weight[layer_index], preferred_element_type=jnp.float32)
    )
    return (hidden.astype(jnp.float32) + branch).astype(jnp.bfloat16)

GELU_LINEAR = 2.0 * math.sqrt(2.0 / math.pi)
GELU_CUBIC = 4.0 * 0.044715 * GELU_LINEAR
GROUP = 8


def gelu_of_half(half):
    inner = half * (GELU_LINEAR + GELU_CUBIC * (half * half))
    return half + half * jnp.tanh(inner)


def encoder_kernel(
    frame_ref,
    patch_ref,
    depth_ref,
    point_ref,
    observe_ref,
    out_ref,
    frame,
    cells,
    spread,
    first,
    second,
    mixed,
    depth_rows,
    point_pair,
    observe,
    frame_sem,
    observe_sem,
):
    height, width = frame_ref.shape
    channels = patch_ref.shape[1]
    rows, cols = height // PATCH, width // PATCH
    lane_groups = width // 128
    group_cols = 128 // PATCH
    pool_cols, pool_rows = cols // POOL, rows // POOL
    halves = 2
    half_height = height // halves
    half_rows = pool_rows // halves

    def frame_copy(index):
        taken = pl.ds(index * half_height, half_height)
        return pltpu.make_async_copy(frame_ref.at[taken], frame.at[taken], frame_sem.at[index])

    def observe_copy(index):
        return pltpu.make_async_copy(
            observe_ref.at[index], observe.at[index], observe_sem.at[index]
        )

    for index in range(halves):
        frame_copy(index).start()

    patch = patch_ref[...].astype(jnp.float32) * 0.5
    blank = jnp.zeros((PATCH, channels), jnp.float32)
    spread[...] = jnp.zeros_like(spread)
    for i in range(PATCH):
        part = patch[i * PATCH : (i + 1) * PATCH]
        block = jnp.concatenate(
            [
                jnp.concatenate([part, blank], axis=1),
                jnp.concatenate([blank, part], axis=1),
            ],
            axis=0,
        ).astype(jnp.bfloat16)
        for n in range(group_cols // 2):
            spread[n, pl.ds(i * 128 + n * 2 * PATCH, 2 * PATCH), :] = block
    square = jnp.zeros((channels, channels), jnp.bfloat16)
    for layer in range(LAYERS):
        point = (point_ref[layer].astype(jnp.float32) * 0.5).astype(jnp.bfloat16)
        point_pair[layer, :channels, :channels] = point
        point_pair[layer, channels:, channels:] = point
        point_pair[layer, :channels, channels:] = square
        point_pair[layer, channels:, :channels] = square
    for layer in range(LAYERS):
        for dr in range(3):
            taps = depth_ref[layer, dr].astype(jnp.float32)
            for dc in range(3):
                depth_rows[(layer * 3 + dr) * 3 + dc] = jnp.broadcast_to(
                    taps[dc : dc + 1], (pool_rows, channels)
                ).astype(jnp.bfloat16)

    for ref in (first, second):
        column = jnp.zeros(ref.shape[1:], jnp.bfloat16)
        ref[0] = column
        ref[cols + 1] = column

    to_row = lax.broadcasted_iota(jnp.int32, (half_height, half_height), 0)
    from_row = lax.broadcasted_iota(jnp.int32, (half_height, half_height), 1)
    place = to_row // half_rows
    source_row = (to_row % half_rows) * (POOL * PATCH) + (place % POOL) * PATCH + place // POOL
    order = jnp.where(from_row == source_row, 1.0, 0.0).astype(jnp.bfloat16)
    for index in range(halves):
        frame_copy(index).wait()
    for index in range(pool_cols):
        observe_copy(index).start()
    for pair in range(lane_groups // 2):
        lanes = slice(pair * 256, (pair + 1) * 256)
        ordered = [
            jnp.dot(
                order,
                frame[h * half_height : (h + 1) * half_height, lanes],
                preferred_element_type=jnp.float32,
            )
            for h in range(halves)
        ]
        for i in range(PATCH):
            for q in range(POOL):
                at = (i * POOL + q) * half_rows
                tile = jnp.concatenate(
                    [part[at : at + half_rows] for part in ordered], axis=0
                ).astype(jnp.bfloat16)
                for g in range(2):
                    cells[
                        pair * 2 + g,
                        q * pool_rows : (q + 1) * pool_rows,
                        i * 128 : (i + 1) * 128,
                    ] = tile[:, g * 128 : (g + 1) * 128]

    sublane = lax.broadcasted_iota(jnp.int32, (pool_rows, channels), 0)

    def store_column(target, column, tiles):
        for q in range(POOL):
            target[column, q + 1] = tiles[q].astype(jnp.bfloat16)
        above = pltpu.roll(tiles[POOL - 1], 1, 0)
        below = pltpu.roll(tiles[0], pool_rows - 1, 0)
        target[column, 0] = jnp.where(sublane == 0, 0.0, above).astype(jnp.bfloat16)
        target[column, POOL + 1] = jnp.where(sublane == pool_rows - 1, 0.0, below).astype(
            jnp.bfloat16
        )

    half_groups = max(lane_groups // 2, 1)

    def embed_step(step, carry):
        n = step // (lane_groups // half_groups)
        part = step % (lane_groups // half_groups)
        taken = cells[pl.ds(part * half_groups, half_groups)].reshape(
            half_groups * rows, PATCH * 128
        )
        half = jnp.dot(taken, spread[n], preferred_element_type=jnp.float32)
        for g in range(half_groups):
            column = (part * half_groups + g) * group_cols + 2 * n + 1
            for o in range(2):
                tiles = [
                    gelu_of_half(
                        half[
                            g * rows + q * pool_rows : g * rows + (q + 1) * pool_rows,
                            o * channels : (o + 1) * channels,
                        ]
                    )
                    for q in range(POOL)
                ]
                store_column(first, column + o, tiles)
        return carry

    lax.fori_loop(0, (group_cols // 2) * (lane_groups // half_groups), embed_step, 0)

    def mix_cells(layer, source, group):
        start = group * GROUP
        weights = [depth_rows[layer * 9 + tap] for tap in range(9)]
        for q in range(POOL):
            sums = [None] * GROUP
            for cc in range(GROUP + 2):
                taken = [source[start + cc, q + dr] for dr in range(3)]
                for dc in range(3):
                    o = cc - dc
                    if 0 <= o < GROUP:
                        term = (
                            taken[0] * weights[dc] + taken[1] * weights[3 + dc]
                        ) + taken[2] * weights[6 + dc]
                        sums[o] = term if sums[o] is None else sums[o] + term
                if cc >= 2:
                    o = cc - 2
                    at = (o // 2) * rows + q * pool_rows
                    mixed[
                        at : at + pool_rows, (o % 2) * channels : (o % 2 + 1) * channels
                    ] = sums[o]

    def mix_channels(layer):
        return jnp.dot(mixed[...], point_pair[layer], preferred_element_type=jnp.float32)

    def updated(source, group, half, o):
        tiles = []
        for q in range(POOL):
            at = (o // 2) * rows + q * pool_rows
            branch = gelu_of_half(
                half[at : at + pool_rows, (o % 2) * channels : (o % 2 + 1) * channels]
            )
            tiles.append(source[group * GROUP + o + 1, q + 1].astype(jnp.float32) + branch)
        return tiles

    def finish(target, source, group, half, carry):
        for o in range(GROUP):
            store_column(target, group * GROUP + o + 1, updated(source, group, half, o))
        return carry

    def finish_pooled(source, group, half, total):
        summed = jnp.zeros((pool_rows, channels), jnp.float32)
        for o in range(GROUP):
            for tile in updated(source, group, half, o):
                summed = summed + tile
        pooled = summed * (1.0 / (POOL * POOL))
        features = jnp.concatenate(
            [jnp.where(sublane == r, pooled, 0.0) for r in range(pool_rows)], axis=1
        ).astype(jnp.bfloat16)
        observe_copy(group).wait()
        return total + jnp.dot(features, observe[group], preferred_element_type=jnp.float32)

    def run_layer(layer, source, finish, carry):
        groups = cols // GROUP
        mix_cells(layer, source, 0)

        def step(group, carry):
            half = mix_channels(layer)
            mix_cells(layer, source, group)
            return finish(source, group - 1, half, carry)

        carry = lax.fori_loop(1, groups, step, carry)
        return finish(source, groups - 1, mix_channels(layer), carry)

    refs = (first, second)
    for layer in range(LAYERS - 1):
        run_layer(
            layer, refs[layer % 2], functools.partial(finish, refs[(layer + 1) % 2]), 0
        )
    total = run_layer(
        LAYERS - 1,
        refs[(LAYERS - 1) % 2],
        finish_pooled,
        jnp.zeros((pool_rows, observe.shape[2]), jnp.float32),
    )
    out_ref[...] = jnp.sum(total, axis=0, keepdims=True)


def encode_whole(frame, patch_weight, depth_weight, point_weight, observe_weight):
    height, width = frame.shape
    channels = patch_weight.shape[1]
    rows, cols = height // PATCH, width // PATCH
    pool_cols, pool_rows, _, components = observe_weight.shape
    observe_weight = observe_weight.reshape(pool_cols, pool_rows * channels, components)
    vmem = pl.BlockSpec(memory_space=pltpu.VMEM)
    anywhere = pl.BlockSpec(memory_space=pl.ANY)
    padded = (cols + 2, POOL + 2, pool_rows, channels)
    return pl.pallas_call(
        encoder_kernel,
        out_shape=jax.ShapeDtypeStruct((1, components), jnp.float32),
        in_specs=[anywhere, vmem, vmem, vmem, anywhere],
        out_specs=vmem,
        scratch_shapes=[
            pltpu.VMEM((height, width), jnp.bfloat16),
            pltpu.VMEM((width // 128, rows, PATCH * 128), jnp.bfloat16),
            pltpu.VMEM((128 // PATCH // 2, PATCH * 128, 2 * channels), jnp.bfloat16),
            pltpu.VMEM(padded, jnp.bfloat16),
            pltpu.VMEM(padded, jnp.bfloat16),
            pltpu.VMEM((GROUP // 2 * rows, 2 * channels), jnp.bfloat16),
            pltpu.VMEM((LAYERS * 9, pool_rows, channels), jnp.bfloat16),
            pltpu.VMEM((LAYERS, 2 * channels, 2 * channels), jnp.bfloat16),
            pltpu.VMEM(observe_weight.shape, jnp.bfloat16),
            pltpu.SemaphoreType.DMA((2,)),
            pltpu.SemaphoreType.DMA((pool_cols,)),
        ],
        compiler_params=pltpu.CompilerParams(vmem_limit_bytes=60 * 1024 * 1024),
        name="encoder",
    )(frame, patch_weight, depth_weight, point_weight, observe_weight)


def complex_times(a, b):
    return (a[0] * b[0] - a[1] * b[1], a[0] * b[1] + a[1] * b[0])


def filter_kernel(
    count,
    observed_ref,
    map_ref,
    decay_ref,
    angle_ref,
    back_decay_ref,
    back_angle_ref,
    out_ref,
    gathered,
    send_sem,
    recv_sem,
):
    me = lax.axis_index("tm")
    barrier = pltpu.get_barrier_semaphore()

    def greet(step, carry):
        pl.semaphore_signal(
            barrier,
            inc=1,
            device_id={"tm": lax.rem(me + step, count)},
            device_id_type=pl.DeviceIdType.MESH,
        )
        return carry

    lax.fori_loop(1, count, greet, 0)

    mode_refs = (decay_ref, angle_ref, back_decay_ref, back_angle_ref)
    modes = decay_ref.shape[1]
    state = 2 * modes
    mode = lax.broadcasted_iota(jnp.int32, (modes, state), 0)
    component = lax.broadcasted_iota(jnp.int32, (modes, state), 1)
    repeat = jnp.where(component // 2 == mode, 1.0, 0.0)
    doubled = jnp.dot(
        jnp.concatenate([ref[...] for ref in mode_refs], axis=0),
        repeat,
        precision=lax.Precision.HIGHEST,
        preferred_element_type=jnp.float32,
    )
    decay, angle, back_decay, back_angle = (doubled[k : k + 1] for k in range(4))
    drive = lax.dot_general(
        observed_ref[...],
        map_ref[...],
        (((1,), (1,)), ((), ())),
        precision=lax.Precision.HIGHEST,
        preferred_element_type=jnp.float32,
    ) * jnp.sqrt(1.0 - decay * decay)
    gathered[pl.ds(me, 1)] = drive.reshape(1, 1, state)
    pl.semaphore_wait(barrier, count - 1)

    def copy_to(step):
        return pltpu.make_async_remote_copy(
            src_ref=gathered.at[me],
            dst_ref=gathered.at[me],
            send_sem=send_sem.at[step],
            recv_sem=recv_sem.at[me],
            device_id={"tm": lax.rem(me + step, count)},
            device_id_type=pl.DeviceIdType.MESH,
        )

    def send(step, carry):
        copy_to(step).start()
        return carry

    lax.fori_loop(1, count, send, 0)

    forward = (decay * jnp.cos(angle), decay * jnp.sin(angle))
    backward = (back_decay * jnp.cos(back_angle), back_decay * jnp.sin(back_angle))
    both = complex_times(forward, backward)
    frame = lax.broadcasted_iota(jnp.int32, (count, state), 0)
    one = (jnp.ones((1, state), jnp.float32), jnp.zeros((1, state), jnp.float32))
    power, partial = one, one
    partial_sums = [one]
    for _ in range(count - 1):
        power = complex_times(power, both)
        partial = (partial[0] + power[0], partial[1] + power[1])
        partial_sums.append(partial)
    last = jnp.maximum(frame, me)
    sums = [jnp.zeros((count, state), jnp.float32) for _ in range(2)]
    for n in range(count):
        for k in range(2):
            sums[k] = jnp.where(last == count - 1 - n, partial_sums[n][k], sums[k])
    away = jnp.abs(frame - me)
    factor = tuple(jnp.where(frame > me, backward[k], forward[k]) for k in range(2))
    gain = tuple(sums)
    bit = 1
    while bit < count:
        taken = complex_times(gain, factor)
        chosen = (away // bit) % 2 == 1
        gain = tuple(jnp.where(chosen, taken[k], gain[k]) for k in range(2))
        factor = complex_times(factor, factor)
        bit = bit * 2
    weight = jnp.sqrt(1.0 - back_decay * back_decay)
    imaginary = lax.broadcasted_iota(jnp.int32, (count, state), 1) % 2 == 1
    direct = gain[0] * weight
    crossed = jnp.where(imaginary, gain[1], -gain[1]) * weight

    def arrive(step, carry):
        source = lax.rem(me + step, count)
        pltpu.make_async_remote_copy(
            src_ref=gathered.at[source],
            dst_ref=gathered.at[source],
            send_sem=send_sem.at[step],
            recv_sem=recv_sem.at[source],
            device_id={"tm": source},
            device_id_type=pl.DeviceIdType.MESH,
        ).wait_recv()
        return carry

    lax.fori_loop(1, count, arrive, 0)
    drives = gathered[...].reshape(count, state)
    partner = jnp.where(
        imaginary, pltpu.roll(drives, 1, 1), pltpu.roll(drives, state - 1, 1)
    )
    out_ref[...] = jnp.sum(direct * drives + crossed * partner, axis=0, keepdims=True)

    def sent(step, carry):
        copy_to(step).wait_send()
        return carry

    lax.fori_loop(1, count, sent, 0)


def smoothed_state(observed, input_map, *modes):
    count = lax.axis_size("tm")
    state = input_map.shape[0]
    vmem = pl.BlockSpec(memory_space=pltpu.VMEM)
    return pl.pallas_call(
        functools.partial(filter_kernel, count),
        out_shape=jax.ShapeDtypeStruct((1, state), jnp.float32),
        in_specs=[vmem] * 6,
        out_specs=vmem,
        scratch_shapes=[
            pltpu.VMEM((count, 1, state), jnp.float32),
            pltpu.SemaphoreType.DMA((count,)),
            pltpu.SemaphoreType.DMA((count,)),
        ],
        compiler_params=pltpu.CompilerParams(collective_id=0, has_side_effects=True),
        name="filters",
    )(observed, input_map, *(mode.reshape(1, -1) for mode in modes))


def encode_tiles(frames, patch_weight, depth_weight, point_weight, observe_weight):
    frame_count, height, width = frames.shape
    grid_rows = height // PATCH
    grid_cols = width // PATCH
    channels = patch_weight.shape[1]
    hidden = embed(frames, patch_weight)
    for layer_index in range(LAYERS):
        widened = with_halo(hidden, (("tile", 2),), 1)
        padded = jnp.pad(widened, ((0, 0), (1, 1), (0, 0), (0, 0)))
        hidden = conv_layer(hidden, padded, depth_weight, point_weight, layer_index)
    pooled = jnp.mean(
        hidden.astype(jnp.float32).reshape(
            frame_count, grid_rows // POOL, POOL, grid_cols // POOL, POOL, channels
        ),
        axis=(2, 4),
    ).astype(jnp.bfloat16)
    features = pooled.transpose(0, 2, 1, 3).reshape(frame_count, -1)
    partial_value = jnp.dot(
        features,
        observe_weight.reshape(-1, observe_weight.shape[-1]),
        preferred_element_type=jnp.float32,
    )
    return lax.psum(partial_value, "tile")


def shards(
    movie_frames,
    patch_weight,
    depth_weight,
    point_weight,
    observe_weight,
    input_map,
    mode_decay,
    mode_angle,
    smooth_decay,
    smooth_angle,
    readout,
):
    tile_count = lax.axis_size("tile")
    encoder = (patch_weight, depth_weight, point_weight, observe_weight)
    if tile_count == 1:
        observed = encode_whole(movie_frames[0], *encoder)
    else:
        observed = encode_tiles(movie_frames, *encoder)
        share = readout.shape[0] // tile_count
        readout = lax.dynamic_slice_in_dim(readout, lax.axis_index("tile") * share, share, 0)
    smoothed = smoothed_state(
        observed, input_map, mode_decay, mode_angle, smooth_decay, smooth_angle
    )
    return jnp.dot(smoothed, readout.T, precision=lax.Precision.HIGHEST)


def solution(mesh):
    placed = (
        P("tm", None, "tile"),
        P(),
        P(),
        P(),
        P("tile", None, None, None),
        P(),
        P(),
        P(),
        P(),
        P(),
        P(),
    )
    return jax.shard_map(
        shards, mesh=mesh, in_specs=placed, out_specs=P("tm", "tile"), check_vma=False
    )
```

```python
import functools
import math

import jax
import jax.numpy as jnp
from jax import lax
from jax.experimental import pallas as pl
from jax.experimental.pallas import tpu as pltpu
from jax.sharding import PartitionSpec as P

PATCH = 8
POOL = 8
LAYERS = 3


def with_halo(x, sides, width):
    for axis, dim in sides:
        size, length = (lax.axis_size(axis), x.shape[dim])
        up = [(i, (i + 1) % size) for i in range(size - 1)]
        down = [(j, i) for i, j in up]
        last = lax.slice_in_dim(x, length - width, length, axis=dim)
        initial = lax.slice_in_dim(x, 0, width, axis=dim)
        before = lax.ppermute(last, axis, up)
        after = lax.ppermute(initial, axis, down)
        x = jnp.concatenate([before, x, after], axis=dim)
    return x


def embed(frames, patch_weight):
    frame_count, height, width = frames.shape
    grid_rows = height // PATCH
    grid_cols = width // PATCH
    patches = (
        frames.reshape(frame_count, grid_rows, PATCH, grid_cols, PATCH)
        .transpose(0, 1, 3, 2, 4)
        .reshape(frame_count, grid_rows, grid_cols, PATCH * PATCH)
    )
    return jax.nn.gelu(jnp.dot(patches, patch_weight, preferred_element_type=jnp.float32)).astype(
        jnp.bfloat16
    )


def conv_layer(hidden, padded, depth_weight, point_weight, layer_index):
    grid_rows = hidden.shape[1]
    grid_cols = hidden.shape[2]
    summed = jnp.zeros(hidden.shape, jnp.float32)
    for row_shift in range(3):
        for col_shift in range(3):
            kernel = depth_weight[layer_index, row_shift, col_shift].astype(jnp.float32)
            summed = (
                summed
                + padded[
                    :, row_shift : row_shift + grid_rows, col_shift : col_shift + grid_cols
                ].astype(jnp.float32)
                * kernel
            )
    depthwise = summed.astype(jnp.bfloat16)
    branch = jax.nn.gelu(
        jnp.dot(depthwise, point_weight[layer_index], preferred_element_type=jnp.float32)
    )
    return (hidden.astype(jnp.float32) + branch).astype(jnp.bfloat16)

GELU_LINEAR = 2.0 * math.sqrt(2.0 / math.pi)
GELU_CUBIC = 4.0 * 0.044715 * GELU_LINEAR
GROUP = 8


def log2(size):
    return size.bit_length() - 1


def gelu_of_half(half):
    inner = half * (GELU_LINEAR + GELU_CUBIC * (half * half))
    return half + half * jnp.tanh(inner)


def encoder_kernel(
    frame_ref,
    patch_ref,
    depth_ref,
    point_ref,
    observe_ref,
    out_ref,
    frame,
    cells,
    spread,
    first,
    second,
    mixed,
    depth_rows,
    point_pair,
    observe,
    frame_sem,
    observe_sem,
):
    height, width = frame_ref.shape
    channels = patch_ref.shape[1]
    rows, cols = height // PATCH, width // PATCH
    lane_groups = width // 128
    group_cols = 128 // PATCH
    pool_cols, pool_rows = cols // POOL, rows // POOL
    halves = 2
    half_height = height // halves
    half_rows = pool_rows // halves

    def frame_copy(index):
        taken = pl.ds(index * half_height, half_height)
        return pltpu.make_async_copy(frame_ref.at[taken], frame.at[taken], frame_sem.at[index])

    def observe_copy(index):
        return pltpu.make_async_copy(
            observe_ref.at[index], observe.at[index], observe_sem.at[index]
        )

    for index in range(halves):
        frame_copy(index).start()

    patch = patch_ref[...].astype(jnp.float32) * 0.5
    blank = jnp.zeros((PATCH, channels), jnp.float32)
    spread[...] = jnp.zeros_like(spread)
    for i in range(PATCH):
        part = patch[i * PATCH : (i + 1) * PATCH]
        block = jnp.concatenate(
            [
                jnp.concatenate([part, blank], axis=1),
                jnp.concatenate([blank, part], axis=1),
            ],
            axis=0,
        ).astype(jnp.bfloat16)
        for n in range(group_cols // 2):
            spread[n, pl.ds(i * 128 + n * 2 * PATCH, 2 * PATCH), :] = block
    square = jnp.zeros((channels, channels), jnp.bfloat16)
    for layer in range(LAYERS):
        point = (point_ref[layer].astype(jnp.float32) * 0.5).astype(jnp.bfloat16)
        point_pair[layer, :channels, :channels] = point
        point_pair[layer, channels:, channels:] = point
        point_pair[layer, :channels, channels:] = square
        point_pair[layer, channels:, :channels] = square
    for layer in range(LAYERS):
        for dr in range(3):
            taps = depth_ref[layer, dr].astype(jnp.float32)
            for dc in range(3):
                depth_rows[(layer * 3 + dr) * 3 + dc] = jnp.broadcast_to(
                    taps[dc : dc + 1], (pool_rows, channels)
                ).astype(jnp.bfloat16)

    for ref in (first, second):
        column = jnp.zeros(ref.shape[1:], jnp.bfloat16)
        ref[0] = column
        ref[cols + 1] = column

    to_row = lax.broadcasted_iota(jnp.int32, (half_height, half_height), 0)
    from_row = lax.broadcasted_iota(jnp.int32, (half_height, half_height), 1)
    place = to_row >> log2(half_rows)
    source_row = (
        ((to_row & (half_rows - 1)) << log2(POOL * PATCH))
        + ((place & (POOL - 1)) << log2(PATCH))
        + (place >> log2(POOL))
    )
    order = jnp.where(from_row == source_row, 1.0, 0.0).astype(jnp.bfloat16)
    for index in range(halves):
        frame_copy(index).wait()
    for index in range(pool_cols):
        observe_copy(index).start()
    for pair in range(lane_groups // 2):
        lanes = slice(pair * 256, (pair + 1) * 256)
        ordered = [
            jnp.dot(
                order,
                frame[h * half_height : (h + 1) * half_height, lanes],
                preferred_element_type=jnp.float32,
            )
            for h in range(halves)
        ]
        for i in range(PATCH):
            for q in range(POOL):
                at = (i * POOL + q) * half_rows
                tile = jnp.concatenate(
                    [part[at : at + half_rows] for part in ordered], axis=0
                ).astype(jnp.bfloat16)
                for g in range(2):
                    cells[
                        pair * 2 + g,
                        q * pool_rows : (q + 1) * pool_rows,
                        i * 128 : (i + 1) * 128,
                    ] = tile[:, g * 128 : (g + 1) * 128]

    sublane = lax.broadcasted_iota(jnp.int32, (pool_rows, channels), 0)

    def store_column(target, column, tiles):
        for q in range(POOL):
            target[column, q + 1] = tiles[q].astype(jnp.bfloat16)
        above = pltpu.roll(tiles[POOL - 1], 1, 0)
        below = pltpu.roll(tiles[0], pool_rows - 1, 0)
        target[column, 0] = jnp.where(sublane == 0, 0.0, above).astype(jnp.bfloat16)
        target[column, POOL + 1] = jnp.where(sublane == pool_rows - 1, 0.0, below).astype(
            jnp.bfloat16
        )

    half_groups = max(lane_groups // 2, 1)

    def embed_step(step, carry):
        n = step // (lane_groups // half_groups)
        part = step % (lane_groups // half_groups)
        taken = cells[pl.ds(part * half_groups, half_groups)].reshape(
            half_groups * rows, PATCH * 128
        )
        half = jnp.dot(taken, spread[n], preferred_element_type=jnp.float32)
        for g in range(half_groups):
            column = (part * half_groups + g) * group_cols + 2 * n + 1
            for o in range(2):
                tiles = [
                    gelu_of_half(
                        half[
                            g * rows + q * pool_rows : g * rows + (q + 1) * pool_rows,
                            o * channels : (o + 1) * channels,
                        ]
                    )
                    for q in range(POOL)
                ]
                store_column(first, column + o, tiles)
        return carry

    lax.fori_loop(0, (group_cols // 2) * (lane_groups // half_groups), embed_step, 0)

    def mix_cells(layer, source, group):
        start = group * GROUP
        weights = [depth_rows[layer * 9 + tap] for tap in range(9)]
        for q in range(POOL):
            sums = [None] * GROUP
            for cc in range(GROUP + 2):
                taken = [source[start + cc, q + dr] for dr in range(3)]
                for dc in range(3):
                    o = cc - dc
                    if 0 <= o < GROUP:
                        term = (
                            taken[0] * weights[dc] + taken[1] * weights[3 + dc]
                        ) + taken[2] * weights[6 + dc]
                        sums[o] = term if sums[o] is None else sums[o] + term
                if cc >= 2:
                    o = cc - 2
                    at = (o // 2) * rows + q * pool_rows
                    mixed[
                        at : at + pool_rows, (o % 2) * channels : (o % 2 + 1) * channels
                    ] = sums[o]

    def mix_channels(layer):
        return jnp.dot(mixed[...], point_pair[layer], preferred_element_type=jnp.float32)

    def updated(source, group, half, o):
        tiles = []
        for q in range(POOL):
            at = (o // 2) * rows + q * pool_rows
            branch = gelu_of_half(
                half[at : at + pool_rows, (o % 2) * channels : (o % 2 + 1) * channels]
            )
            tiles.append(source[group * GROUP + o + 1, q + 1].astype(jnp.float32) + branch)
        return tiles

    def finish(target, source, group, half, carry):
        for o in range(GROUP):
            store_column(target, group * GROUP + o + 1, updated(source, group, half, o))
        return carry

    def finish_pooled(source, group, half, total):
        summed = jnp.zeros((pool_rows, channels), jnp.float32)
        for o in range(GROUP):
            for tile in updated(source, group, half, o):
                summed = summed + tile
        pooled = summed * (1.0 / (POOL * POOL))
        features = jnp.concatenate(
            [jnp.where(sublane == r, pooled, 0.0) for r in range(pool_rows)], axis=1
        ).astype(jnp.bfloat16)
        observe_copy(group).wait()
        return total + jnp.dot(features, observe[group], preferred_element_type=jnp.float32)

    def run_layer(layer, source, finish, carry):
        groups = cols // GROUP
        mix_cells(layer, source, 0)

        def step(group, carry):
            half = mix_channels(layer)
            mix_cells(layer, source, group)
            return finish(source, group - 1, half, carry)

        carry = lax.fori_loop(1, groups, step, carry)
        return finish(source, groups - 1, mix_channels(layer), carry)

    refs = (first, second)
    for layer in range(LAYERS - 1):
        run_layer(
            layer, refs[layer % 2], functools.partial(finish, refs[(layer + 1) % 2]), 0
        )
    total = run_layer(
        LAYERS - 1,
        refs[(LAYERS - 1) % 2],
        finish_pooled,
        jnp.zeros((pool_rows, observe.shape[2]), jnp.float32),
    )
    out_ref[...] = jnp.sum(total, axis=0, keepdims=True)


def encode_whole(frame, patch_weight, depth_weight, point_weight, observe_weight):
    height, width = frame.shape
    channels = patch_weight.shape[1]
    rows, cols = height // PATCH, width // PATCH
    pool_cols, pool_rows, _, components = observe_weight.shape
    observe_weight = observe_weight.reshape(pool_cols, pool_rows * channels, components)
    vmem = pl.BlockSpec(memory_space=pltpu.VMEM)
    anywhere = pl.BlockSpec(memory_space=pl.ANY)
    padded = (cols + 2, POOL + 2, pool_rows, channels)
    return pl.pallas_call(
        encoder_kernel,
        out_shape=jax.ShapeDtypeStruct((1, components), jnp.float32),
        in_specs=[anywhere, vmem, vmem, vmem, anywhere],
        out_specs=vmem,
        scratch_shapes=[
            pltpu.VMEM((height, width), jnp.bfloat16),
            pltpu.VMEM((width // 128, rows, PATCH * 128), jnp.bfloat16),
            pltpu.VMEM((128 // PATCH // 2, PATCH * 128, 2 * channels), jnp.bfloat16),
            pltpu.VMEM(padded, jnp.bfloat16),
            pltpu.VMEM(padded, jnp.bfloat16),
            pltpu.VMEM((GROUP // 2 * rows, 2 * channels), jnp.bfloat16),
            pltpu.VMEM((LAYERS * 9, pool_rows, channels), jnp.bfloat16),
            pltpu.VMEM((LAYERS, 2 * channels, 2 * channels), jnp.bfloat16),
            pltpu.VMEM(observe_weight.shape, jnp.bfloat16),
            pltpu.SemaphoreType.DMA((2,)),
            pltpu.SemaphoreType.DMA((pool_cols,)),
        ],
        compiler_params=pltpu.CompilerParams(vmem_limit_bytes=60 * 1024 * 1024),
        name="encoder",
    )(frame, patch_weight, depth_weight, point_weight, observe_weight)


def complex_times(a, b):
    return (a[0] * b[0] - a[1] * b[1], a[0] * b[1] + a[1] * b[0])


def filter_kernel(
    count,
    observed_ref,
    map_ref,
    decay_ref,
    angle_ref,
    back_decay_ref,
    back_angle_ref,
    out_ref,
    gathered,
    send_sem,
    recv_sem,
):
    me = lax.axis_index("tm")
    barrier = pltpu.get_barrier_semaphore()

    def greet(step, carry):
        pl.semaphore_signal(
            barrier,
            inc=1,
            device_id={"tm": lax.rem(me + step, count)},
            device_id_type=pl.DeviceIdType.MESH,
        )
        return carry

    lax.fori_loop(1, count, greet, 0)

    mode_refs = (decay_ref, angle_ref, back_decay_ref, back_angle_ref)
    modes = decay_ref.shape[1]
    state = 2 * modes
    mode = lax.broadcasted_iota(jnp.int32, (modes, state), 0)
    component = lax.broadcasted_iota(jnp.int32, (modes, state), 1)
    repeat = jnp.where(component >> 1 == mode, 1.0, 0.0)
    doubled = jnp.dot(
        jnp.concatenate([ref[...] for ref in mode_refs], axis=0),
        repeat,
        precision=lax.Precision.HIGHEST,
        preferred_element_type=jnp.float32,
    )
    decay, angle, back_decay, back_angle = (doubled[k : k + 1] for k in range(4))
    drive = lax.dot_general(
        observed_ref[...],
        map_ref[...],
        (((1,), (1,)), ((), ())),
        precision=lax.Precision.HIGHEST,
        preferred_element_type=jnp.float32,
    ) * jnp.sqrt(1.0 - decay * decay)
    gathered[pl.ds(me, 1)] = drive.reshape(1, 1, state)
    pl.semaphore_wait(barrier, count - 1)

    def copy_to(step):
        return pltpu.make_async_remote_copy(
            src_ref=gathered.at[me],
            dst_ref=gathered.at[me],
            send_sem=send_sem.at[step],
            recv_sem=recv_sem.at[me],
            device_id={"tm": lax.rem(me + step, count)},
            device_id_type=pl.DeviceIdType.MESH,
        )

    def send(step, carry):
        copy_to(step).start()
        return carry

    lax.fori_loop(1, count, send, 0)

    forward = (decay * jnp.cos(angle), decay * jnp.sin(angle))
    backward = (back_decay * jnp.cos(back_angle), back_decay * jnp.sin(back_angle))
    both = complex_times(forward, backward)
    frame = lax.broadcasted_iota(jnp.int32, (count, state), 0)
    one = (jnp.ones((1, state), jnp.float32), jnp.zeros((1, state), jnp.float32))
    power, partial = one, one
    partial_sums = [one]
    for _ in range(count - 1):
        power = complex_times(power, both)
        partial = (partial[0] + power[0], partial[1] + power[1])
        partial_sums.append(partial)
    last = jnp.maximum(frame, me)
    sums = [jnp.zeros((count, state), jnp.float32) for _ in range(2)]
    for n in range(count):
        for k in range(2):
            sums[k] = jnp.where(last == count - 1 - n, partial_sums[n][k], sums[k])
    away = jnp.abs(frame - me)
    factor = tuple(jnp.where(frame > me, backward[k], forward[k]) for k in range(2))
    gain = tuple(sums)
    bit = 1
    while bit < count:
        taken = complex_times(gain, factor)
        chosen = (away & bit) != 0
        gain = tuple(jnp.where(chosen, taken[k], gain[k]) for k in range(2))
        factor = complex_times(factor, factor)
        bit = bit * 2
    weight = jnp.sqrt(1.0 - back_decay * back_decay)
    imaginary = (lax.broadcasted_iota(jnp.int32, (count, state), 1) & 1) == 1
    direct = gain[0] * weight
    crossed = jnp.where(imaginary, gain[1], -gain[1]) * weight

    def arrive(step, carry):
        source = lax.rem(me + step, count)
        pltpu.make_async_remote_copy(
            src_ref=gathered.at[source],
            dst_ref=gathered.at[source],
            send_sem=send_sem.at[step],
            recv_sem=recv_sem.at[source],
            device_id={"tm": source},
            device_id_type=pl.DeviceIdType.MESH,
        ).wait_recv()
        return carry

    lax.fori_loop(1, count, arrive, 0)
    drives = gathered[...].reshape(count, state)
    partner = jnp.where(
        imaginary, pltpu.roll(drives, 1, 1), pltpu.roll(drives, state - 1, 1)
    )
    out_ref[...] = jnp.sum(direct * drives + crossed * partner, axis=0, keepdims=True)

    def sent(step, carry):
        copy_to(step).wait_send()
        return carry

    lax.fori_loop(1, count, sent, 0)


def smoothed_state(observed, input_map, *modes):
    count = lax.axis_size("tm")
    state = input_map.shape[0]
    vmem = pl.BlockSpec(memory_space=pltpu.VMEM)
    return pl.pallas_call(
        functools.partial(filter_kernel, count),
        out_shape=jax.ShapeDtypeStruct((1, state), jnp.float32),
        in_specs=[vmem] * 6,
        out_specs=vmem,
        scratch_shapes=[
            pltpu.VMEM((count, 1, state), jnp.float32),
            pltpu.SemaphoreType.DMA((count,)),
            pltpu.SemaphoreType.DMA((count,)),
        ],
        compiler_params=pltpu.CompilerParams(collective_id=0, has_side_effects=True),
        name="filters",
    )(observed, input_map, *(mode.reshape(1, -1) for mode in modes))


def encode_tiles(frames, patch_weight, depth_weight, point_weight, observe_weight):
    frame_count, height, width = frames.shape
    grid_rows = height // PATCH
    grid_cols = width // PATCH
    channels = patch_weight.shape[1]
    hidden = embed(frames, patch_weight)
    for layer_index in range(LAYERS):
        widened = with_halo(hidden, (("tile", 2),), 1)
        padded = jnp.pad(widened, ((0, 0), (1, 1), (0, 0), (0, 0)))
        hidden = conv_layer(hidden, padded, depth_weight, point_weight, layer_index)
    pooled = jnp.mean(
        hidden.astype(jnp.float32).reshape(
            frame_count, grid_rows // POOL, POOL, grid_cols // POOL, POOL, channels
        ),
        axis=(2, 4),
    ).astype(jnp.bfloat16)
    features = pooled.transpose(0, 2, 1, 3).reshape(frame_count, -1)
    partial_value = jnp.dot(
        features,
        observe_weight.reshape(-1, observe_weight.shape[-1]),
        preferred_element_type=jnp.float32,
    )
    return lax.psum(partial_value, "tile")


def shards(
    movie_frames,
    patch_weight,
    depth_weight,
    point_weight,
    observe_weight,
    input_map,
    mode_decay,
    mode_angle,
    smooth_decay,
    smooth_angle,
    readout,
):
    tile_count = lax.axis_size("tile")
    encoder = (patch_weight, depth_weight, point_weight, observe_weight)
    if tile_count == 1:
        observed = encode_whole(movie_frames[0], *encoder)
    else:
        observed = encode_tiles(movie_frames, *encoder)
        share = readout.shape[0] // tile_count
        readout = lax.dynamic_slice_in_dim(readout, lax.axis_index("tile") * share, share, 0)
    smoothed = smoothed_state(
        observed, input_map, mode_decay, mode_angle, smooth_decay, smooth_angle
    )
    return jnp.dot(smoothed, readout.T, precision=lax.Precision.HIGHEST)


def solution(mesh):
    placed = (
        P("tm", None, "tile"),
        P(),
        P(),
        P(),
        P("tile", None, None, None),
        P(),
        P(),
        P(),
        P(),
        P(),
        P(),
    )
    return jax.shard_map(
        shards, mesh=mesh, in_specs=placed, out_specs=P("tm", "tile"), check_vma=False
    )
```

```python
import functools
import math

import jax
import jax.numpy as jnp
from jax import lax
from jax.experimental import pallas as pl
from jax.experimental.pallas import tpu as pltpu
from jax.sharding import PartitionSpec as P

PATCH = 8
POOL = 8
LAYERS = 3


def with_halo(x, sides, width):
    for axis, dim in sides:
        size, length = (lax.axis_size(axis), x.shape[dim])
        up = [(i, (i + 1) % size) for i in range(size - 1)]
        down = [(j, i) for i, j in up]
        last = lax.slice_in_dim(x, length - width, length, axis=dim)
        initial = lax.slice_in_dim(x, 0, width, axis=dim)
        before = lax.ppermute(last, axis, up)
        after = lax.ppermute(initial, axis, down)
        x = jnp.concatenate([before, x, after], axis=dim)
    return x


def embed(frames, patch_weight):
    frame_count, height, width = frames.shape
    grid_rows = height // PATCH
    grid_cols = width // PATCH
    patches = (
        frames.reshape(frame_count, grid_rows, PATCH, grid_cols, PATCH)
        .transpose(0, 1, 3, 2, 4)
        .reshape(frame_count, grid_rows, grid_cols, PATCH * PATCH)
    )
    return jax.nn.gelu(jnp.dot(patches, patch_weight, preferred_element_type=jnp.float32)).astype(
        jnp.bfloat16
    )


def conv_layer(hidden, padded, depth_weight, point_weight, layer_index):
    grid_rows = hidden.shape[1]
    grid_cols = hidden.shape[2]
    summed = jnp.zeros(hidden.shape, jnp.float32)
    for row_shift in range(3):
        for col_shift in range(3):
            kernel = depth_weight[layer_index, row_shift, col_shift].astype(jnp.float32)
            summed = (
                summed
                + padded[
                    :, row_shift : row_shift + grid_rows, col_shift : col_shift + grid_cols
                ].astype(jnp.float32)
                * kernel
            )
    depthwise = summed.astype(jnp.bfloat16)
    branch = jax.nn.gelu(
        jnp.dot(depthwise, point_weight[layer_index], preferred_element_type=jnp.float32)
    )
    return (hidden.astype(jnp.float32) + branch).astype(jnp.bfloat16)

GELU_LINEAR = 2.0 * math.sqrt(2.0 / math.pi)
GELU_CUBIC = 4.0 * 0.044715 * GELU_LINEAR
GROUP = 8


def log2(size):
    return size.bit_length() - 1


def gelu_of_half(half):
    inner = half * (GELU_LINEAR + GELU_CUBIC * (half * half))
    return half + half * jnp.tanh(inner)


def encoder_kernel(
    frame_ref,
    patch_ref,
    depth_ref,
    point_ref,
    observe_ref,
    out_ref,
    frame,
    cells,
    spread,
    first,
    second,
    mixed,
    depth_rows,
    point_pair,
    observe,
    frame_sem,
    observe_sem,
):
    height, width = frame_ref.shape
    channels = patch_ref.shape[1]
    rows, cols = height // PATCH, width // PATCH
    lane_groups = width // 128
    group_cols = 128 // PATCH
    pool_cols, pool_rows = cols // POOL, rows // POOL
    halves = 2
    half_height = height // halves
    half_rows = pool_rows // halves

    def frame_copy(index):
        taken = pl.ds(index * half_height, half_height)
        return pltpu.make_async_copy(frame_ref.at[taken], frame.at[taken], frame_sem.at[index])

    def observe_copy(index):
        return pltpu.make_async_copy(
            observe_ref.at[index], observe.at[index], observe_sem.at[index]
        )

    for index in range(halves):
        frame_copy(index).start()

    patch = patch_ref[...].astype(jnp.float32) * 0.5
    blank = jnp.zeros((PATCH, channels), jnp.float32)
    spread[...] = jnp.zeros_like(spread)
    for i in range(PATCH):
        part = patch[i * PATCH : (i + 1) * PATCH]
        block = jnp.concatenate(
            [
                jnp.concatenate([part, blank], axis=1),
                jnp.concatenate([blank, part], axis=1),
            ],
            axis=0,
        ).astype(jnp.bfloat16)
        for n in range(group_cols // 2):
            spread[n, pl.ds(i * 128 + n * 2 * PATCH, 2 * PATCH), :] = block
    square = jnp.zeros((channels, channels), jnp.bfloat16)
    for layer in range(LAYERS):
        point = (point_ref[layer].astype(jnp.float32) * 0.5).astype(jnp.bfloat16)
        point_pair[layer, :channels, :channels] = point
        point_pair[layer, channels:, channels:] = point
        point_pair[layer, :channels, channels:] = square
        point_pair[layer, channels:, :channels] = square
    for layer in range(LAYERS):
        for dr in range(3):
            taps = depth_ref[layer, dr].astype(jnp.float32)
            for dc in range(3):
                depth_rows[(layer * 3 + dr) * 3 + dc] = jnp.broadcast_to(
                    taps[dc : dc + 1], (pool_rows, channels)
                ).astype(jnp.bfloat16)

    for ref in (first, second):
        column = jnp.zeros(ref.shape[1:], jnp.bfloat16)
        ref[0] = column
        ref[cols + 1] = column

    to_row = lax.broadcasted_iota(jnp.int32, (half_height, half_height), 0)
    from_row = lax.broadcasted_iota(jnp.int32, (half_height, half_height), 1)
    place = to_row >> log2(half_rows)
    source_row = (
        ((to_row & (half_rows - 1)) << log2(POOL * PATCH))
        + ((place & (POOL - 1)) << log2(PATCH))
        + (place >> log2(POOL))
    )
    order = jnp.where(from_row == source_row, 1.0, 0.0).astype(jnp.bfloat16)
    for index in range(halves):
        frame_copy(index).wait()
    for index in range(pool_cols):
        observe_copy(index).start()
    for pair in range(lane_groups // 2):
        lanes = slice(pair * 256, (pair + 1) * 256)
        ordered = [
            jnp.dot(
                order,
                frame[h * half_height : (h + 1) * half_height, lanes],
                preferred_element_type=jnp.float32,
            )
            for h in range(halves)
        ]
        for i in range(PATCH):
            for q in range(POOL):
                at = (i * POOL + q) * half_rows
                tile = jnp.concatenate(
                    [part[at : at + half_rows] for part in ordered], axis=0
                ).astype(jnp.bfloat16)
                for g in range(2):
                    cells[
                        pair * 2 + g,
                        q * pool_rows : (q + 1) * pool_rows,
                        i * 128 : (i + 1) * 128,
                    ] = tile[:, g * 128 : (g + 1) * 128]

    sublane = lax.broadcasted_iota(jnp.int32, (pool_rows, channels), 0)

    def store_column(target, column, tiles):
        for q in range(POOL):
            target[column, q + 1] = tiles[q].astype(jnp.bfloat16)
        above = pltpu.roll(tiles[POOL - 1], 1, 0)
        below = pltpu.roll(tiles[0], pool_rows - 1, 0)
        target[column, 0] = jnp.where(sublane == 0, 0.0, above).astype(jnp.bfloat16)
        target[column, POOL + 1] = jnp.where(sublane == pool_rows - 1, 0.0, below).astype(
            jnp.bfloat16
        )

    half_groups = max(lane_groups // 2, 1)

    def embed_step(step, carry):
        n = step // (lane_groups // half_groups)
        part = step % (lane_groups // half_groups)
        taken = cells[pl.ds(part * half_groups, half_groups)].reshape(
            half_groups * rows, PATCH * 128
        )
        half = jnp.dot(taken, spread[n], preferred_element_type=jnp.float32)
        for g in range(half_groups):
            column = (part * half_groups + g) * group_cols + 2 * n + 1
            for o in range(2):
                tiles = [
                    gelu_of_half(
                        half[
                            g * rows + q * pool_rows : g * rows + (q + 1) * pool_rows,
                            o * channels : (o + 1) * channels,
                        ]
                    )
                    for q in range(POOL)
                ]
                store_column(first, column + o, tiles)
        return carry

    lax.fori_loop(0, (group_cols // 2) * (lane_groups // half_groups), embed_step, 0)

    def mix_cells(layer, source, group):
        start = group * GROUP
        weights = [depth_rows[layer * 9 + tap] for tap in range(9)]
        for q in range(POOL):
            sums = [None] * GROUP
            for cc in range(GROUP + 2):
                taken = [source[start + cc, q + dr] for dr in range(3)]
                for dc in range(3):
                    o = cc - dc
                    if 0 <= o < GROUP:
                        term = (
                            taken[0] * weights[dc] + taken[1] * weights[3 + dc]
                        ) + taken[2] * weights[6 + dc]
                        sums[o] = term if sums[o] is None else sums[o] + term
                if cc >= 2:
                    o = cc - 2
                    at = (o // 2) * rows + q * pool_rows
                    mixed[
                        at : at + pool_rows, (o % 2) * channels : (o % 2 + 1) * channels
                    ] = sums[o]

    def mix_channels(layer):
        return jnp.dot(mixed[...], point_pair[layer], preferred_element_type=jnp.float32)

    def updated(source, group, half, o):
        tiles = []
        for q in range(POOL):
            at = (o // 2) * rows + q * pool_rows
            branch = gelu_of_half(
                half[at : at + pool_rows, (o % 2) * channels : (o % 2 + 1) * channels]
            )
            tiles.append(source[group * GROUP + o + 1, q + 1].astype(jnp.float32) + branch)
        return tiles

    def finish(target, source, group, half, carry):
        for o in range(GROUP):
            store_column(target, group * GROUP + o + 1, updated(source, group, half, o))
        return carry

    def finish_pooled(source, group, half, total):
        summed = jnp.zeros((pool_rows, channels), jnp.float32)
        for o in range(GROUP):
            for tile in updated(source, group, half, o):
                summed = summed + tile
        pooled = summed * (1.0 / (POOL * POOL))
        features = jnp.concatenate(
            [jnp.where(sublane == r, pooled, 0.0) for r in range(pool_rows)], axis=1
        ).astype(jnp.bfloat16)
        observe_copy(group).wait()
        return total + jnp.dot(features, observe[group], preferred_element_type=jnp.float32)

    def run_layer(layer, source, finish, carry):
        def step(group, carry):
            mix_cells(layer, source, group)
            return finish(source, group, mix_channels(layer), carry)

        return lax.fori_loop(0, cols // GROUP, step, carry)

    refs = (first, second)
    for layer in range(LAYERS - 1):
        run_layer(
            layer, refs[layer % 2], functools.partial(finish, refs[(layer + 1) % 2]), 0
        )
    total = run_layer(
        LAYERS - 1,
        refs[(LAYERS - 1) % 2],
        finish_pooled,
        jnp.zeros((pool_rows, observe.shape[2]), jnp.float32),
    )
    out_ref[...] = jnp.sum(total, axis=0, keepdims=True)


def encode_whole(frame, patch_weight, depth_weight, point_weight, observe_weight):
    height, width = frame.shape
    channels = patch_weight.shape[1]
    rows, cols = height // PATCH, width // PATCH
    pool_cols, pool_rows, _, components = observe_weight.shape
    observe_weight = observe_weight.reshape(pool_cols, pool_rows * channels, components)
    vmem = pl.BlockSpec(memory_space=pltpu.VMEM)
    anywhere = pl.BlockSpec(memory_space=pl.ANY)
    padded = (cols + 2, POOL + 2, pool_rows, channels)
    return pl.pallas_call(
        encoder_kernel,
        out_shape=jax.ShapeDtypeStruct((1, components), jnp.float32),
        in_specs=[anywhere, vmem, vmem, vmem, anywhere],
        out_specs=vmem,
        scratch_shapes=[
            pltpu.VMEM((height, width), jnp.bfloat16),
            pltpu.VMEM((width // 128, rows, PATCH * 128), jnp.bfloat16),
            pltpu.VMEM((128 // PATCH // 2, PATCH * 128, 2 * channels), jnp.bfloat16),
            pltpu.VMEM(padded, jnp.bfloat16),
            pltpu.VMEM(padded, jnp.bfloat16),
            pltpu.VMEM((GROUP // 2 * rows, 2 * channels), jnp.bfloat16),
            pltpu.VMEM((LAYERS * 9, pool_rows, channels), jnp.bfloat16),
            pltpu.VMEM((LAYERS, 2 * channels, 2 * channels), jnp.bfloat16),
            pltpu.VMEM(observe_weight.shape, jnp.bfloat16),
            pltpu.SemaphoreType.DMA((2,)),
            pltpu.SemaphoreType.DMA((pool_cols,)),
        ],
        compiler_params=pltpu.CompilerParams(vmem_limit_bytes=60 * 1024 * 1024),
        name="encoder",
    )(frame, patch_weight, depth_weight, point_weight, observe_weight)


def complex_times(a, b):
    return (a[0] * b[0] - a[1] * b[1], a[0] * b[1] + a[1] * b[0])


def filter_kernel(
    count,
    observed_ref,
    map_ref,
    decay_ref,
    angle_ref,
    back_decay_ref,
    back_angle_ref,
    out_ref,
    gathered,
    send_sem,
    recv_sem,
):
    me = lax.axis_index("tm")
    barrier = pltpu.get_barrier_semaphore()

    def greet(step, carry):
        pl.semaphore_signal(
            barrier,
            inc=1,
            device_id={"tm": lax.rem(me + step, count)},
            device_id_type=pl.DeviceIdType.MESH,
        )
        return carry

    lax.fori_loop(1, count, greet, 0)

    mode_refs = (decay_ref, angle_ref, back_decay_ref, back_angle_ref)
    modes = decay_ref.shape[1]
    state = 2 * modes
    mode = lax.broadcasted_iota(jnp.int32, (modes, state), 0)
    component = lax.broadcasted_iota(jnp.int32, (modes, state), 1)
    repeat = jnp.where(component >> 1 == mode, 1.0, 0.0)
    doubled = jnp.dot(
        jnp.concatenate([ref[...] for ref in mode_refs], axis=0),
        repeat,
        precision=lax.Precision.HIGHEST,
        preferred_element_type=jnp.float32,
    )
    decay, angle, back_decay, back_angle = (doubled[k : k + 1] for k in range(4))
    drive = lax.dot_general(
        observed_ref[...],
        map_ref[...],
        (((1,), (1,)), ((), ())),
        precision=lax.Precision.HIGHEST,
        preferred_element_type=jnp.float32,
    ) * jnp.sqrt(1.0 - decay * decay)
    gathered[pl.ds(me, 1)] = drive.reshape(1, 1, state)
    pl.semaphore_wait(barrier, count - 1)

    def copy_to(step):
        return pltpu.make_async_remote_copy(
            src_ref=gathered.at[me],
            dst_ref=gathered.at[me],
            send_sem=send_sem.at[step],
            recv_sem=recv_sem.at[me],
            device_id={"tm": lax.rem(me + step, count)},
            device_id_type=pl.DeviceIdType.MESH,
        )

    def send(step, carry):
        copy_to(step).start()
        return carry

    lax.fori_loop(1, count, send, 0)

    forward = (decay * jnp.cos(angle), decay * jnp.sin(angle))
    backward = (back_decay * jnp.cos(back_angle), back_decay * jnp.sin(back_angle))
    both = complex_times(forward, backward)
    frame = lax.broadcasted_iota(jnp.int32, (count, state), 0)
    one = (jnp.ones((1, state), jnp.float32), jnp.zeros((1, state), jnp.float32))
    power, partial = one, one
    partial_sums = [one]
    for _ in range(count - 1):
        power = complex_times(power, both)
        partial = (partial[0] + power[0], partial[1] + power[1])
        partial_sums.append(partial)
    last = jnp.maximum(frame, me)
    sums = [jnp.zeros((count, state), jnp.float32) for _ in range(2)]
    for n in range(count):
        for k in range(2):
            sums[k] = jnp.where(last == count - 1 - n, partial_sums[n][k], sums[k])
    away = jnp.abs(frame - me)
    factor = tuple(jnp.where(frame > me, backward[k], forward[k]) for k in range(2))
    gain = tuple(sums)
    bit = 1
    while bit < count:
        taken = complex_times(gain, factor)
        chosen = (away & bit) != 0
        gain = tuple(jnp.where(chosen, taken[k], gain[k]) for k in range(2))
        factor = complex_times(factor, factor)
        bit = bit * 2
    weight = jnp.sqrt(1.0 - back_decay * back_decay)
    imaginary = (lax.broadcasted_iota(jnp.int32, (count, state), 1) & 1) == 1
    direct = gain[0] * weight
    crossed = jnp.where(imaginary, gain[1], -gain[1]) * weight

    def arrive(step, carry):
        source = lax.rem(me + step, count)
        pltpu.make_async_remote_copy(
            src_ref=gathered.at[source],
            dst_ref=gathered.at[source],
            send_sem=send_sem.at[step],
            recv_sem=recv_sem.at[source],
            device_id={"tm": source},
            device_id_type=pl.DeviceIdType.MESH,
        ).wait_recv()
        return carry

    lax.fori_loop(1, count, arrive, 0)
    drives = gathered[...].reshape(count, state)
    partner = jnp.where(
        imaginary, pltpu.roll(drives, 1, 1), pltpu.roll(drives, state - 1, 1)
    )
    out_ref[...] = jnp.sum(direct * drives + crossed * partner, axis=0, keepdims=True)

    def sent(step, carry):
        copy_to(step).wait_send()
        return carry

    lax.fori_loop(1, count, sent, 0)


def smoothed_state(observed, input_map, *modes):
    count = lax.axis_size("tm")
    state = input_map.shape[0]
    vmem = pl.BlockSpec(memory_space=pltpu.VMEM)
    return pl.pallas_call(
        functools.partial(filter_kernel, count),
        out_shape=jax.ShapeDtypeStruct((1, state), jnp.float32),
        in_specs=[vmem] * 6,
        out_specs=vmem,
        scratch_shapes=[
            pltpu.VMEM((count, 1, state), jnp.float32),
            pltpu.SemaphoreType.DMA((count,)),
            pltpu.SemaphoreType.DMA((count,)),
        ],
        compiler_params=pltpu.CompilerParams(collective_id=0, has_side_effects=True),
        name="filters",
    )(observed, input_map, *(mode.reshape(1, -1) for mode in modes))


def encode_tiles(frames, patch_weight, depth_weight, point_weight, observe_weight):
    frame_count, height, width = frames.shape
    grid_rows = height // PATCH
    grid_cols = width // PATCH
    channels = patch_weight.shape[1]
    hidden = embed(frames, patch_weight)
    for layer_index in range(LAYERS):
        widened = with_halo(hidden, (("tile", 2),), 1)
        padded = jnp.pad(widened, ((0, 0), (1, 1), (0, 0), (0, 0)))
        hidden = conv_layer(hidden, padded, depth_weight, point_weight, layer_index)
    pooled = jnp.mean(
        hidden.astype(jnp.float32).reshape(
            frame_count, grid_rows // POOL, POOL, grid_cols // POOL, POOL, channels
        ),
        axis=(2, 4),
    ).astype(jnp.bfloat16)
    features = pooled.transpose(0, 2, 1, 3).reshape(frame_count, -1)
    partial_value = jnp.dot(
        features,
        observe_weight.reshape(-1, observe_weight.shape[-1]),
        preferred_element_type=jnp.float32,
    )
    return lax.psum(partial_value, "tile")


def shards(
    movie_frames,
    patch_weight,
    depth_weight,
    point_weight,
    observe_weight,
    input_map,
    mode_decay,
    mode_angle,
    smooth_decay,
    smooth_angle,
    readout,
):
    tile_count = lax.axis_size("tile")
    encoder = (patch_weight, depth_weight, point_weight, observe_weight)
    if tile_count == 1:
        observed = encode_whole(movie_frames[0], *encoder)
    else:
        observed = encode_tiles(movie_frames, *encoder)
        share = readout.shape[0] // tile_count
        readout = lax.dynamic_slice_in_dim(readout, lax.axis_index("tile") * share, share, 0)
    smoothed = smoothed_state(
        observed, input_map, mode_decay, mode_angle, smooth_decay, smooth_angle
    )
    return jnp.dot(smoothed, readout.T, precision=lax.Precision.HIGHEST)


def solution(mesh):
    placed = (
        P("tm", None, "tile"),
        P(),
        P(),
        P(),
        P("tile", None, None, None),
        P(),
        P(),
        P(),
        P(),
        P(),
        P(),
    )
    return jax.shard_map(
        shards, mesh=mesh, in_specs=placed, out_specs=P("tm", "tile"), check_vma=False
    )
```

```python
import functools
import math

import jax
import jax.numpy as jnp
from jax import lax
from jax.experimental import pallas as pl
from jax.experimental.pallas import tpu as pltpu
from jax.sharding import PartitionSpec as P

PATCH = 8
POOL = 8
LAYERS = 3


def with_halo(x, sides, width):
    for axis, dim in sides:
        size, length = (lax.axis_size(axis), x.shape[dim])
        up = [(i, (i + 1) % size) for i in range(size - 1)]
        down = [(j, i) for i, j in up]
        last = lax.slice_in_dim(x, length - width, length, axis=dim)
        initial = lax.slice_in_dim(x, 0, width, axis=dim)
        before = lax.ppermute(last, axis, up)
        after = lax.ppermute(initial, axis, down)
        x = jnp.concatenate([before, x, after], axis=dim)
    return x


def embed(frames, patch_weight):
    frame_count, height, width = frames.shape
    grid_rows = height // PATCH
    grid_cols = width // PATCH
    patches = (
        frames.reshape(frame_count, grid_rows, PATCH, grid_cols, PATCH)
        .transpose(0, 1, 3, 2, 4)
        .reshape(frame_count, grid_rows, grid_cols, PATCH * PATCH)
    )
    return jax.nn.gelu(jnp.dot(patches, patch_weight, preferred_element_type=jnp.float32)).astype(
        jnp.bfloat16
    )


def conv_layer(hidden, padded, depth_weight, point_weight, layer_index):
    grid_rows = hidden.shape[1]
    grid_cols = hidden.shape[2]
    summed = jnp.zeros(hidden.shape, jnp.float32)
    for row_shift in range(3):
        for col_shift in range(3):
            kernel = depth_weight[layer_index, row_shift, col_shift].astype(jnp.float32)
            summed = (
                summed
                + padded[
                    :, row_shift : row_shift + grid_rows, col_shift : col_shift + grid_cols
                ].astype(jnp.float32)
                * kernel
            )
    depthwise = summed.astype(jnp.bfloat16)
    branch = jax.nn.gelu(
        jnp.dot(depthwise, point_weight[layer_index], preferred_element_type=jnp.float32)
    )
    return (hidden.astype(jnp.float32) + branch).astype(jnp.bfloat16)

GELU_LINEAR = 2.0 * math.sqrt(2.0 / math.pi)
GELU_CUBIC = 4.0 * 0.044715 * GELU_LINEAR
EDGE = 8
GROUP = 8
STRIP = 16


def gelu_of_half(half):
    inner = half * (GELU_LINEAR + GELU_CUBIC * (half * half))
    return half + half * jnp.tanh(inner)


def encoder_kernel(
    frame_ref,
    patch_ref,
    depth_ref,
    point_ref,
    observe_ref,
    out_ref,
    cells,
    spread,
    first,
    second,
    mixed,
    depth_rows,
    point_pair,
    observe,
    observe_sem,
):
    height, width = frame_ref.shape
    channels = patch_ref.shape[1]
    rows, cols = height // PATCH, width // PATCH
    lane_groups = width // 128
    group_cols = 128 // PATCH
    pool_cols, pool_rows = cols // POOL, rows // POOL

    def observe_copy(index):
        return pltpu.make_async_copy(
            observe_ref.at[index], observe.at[index], observe_sem.at[index]
        )

    for index in range(pool_cols):
        observe_copy(index).start()

    patch = patch_ref[...].astype(jnp.float32) * 0.5
    blank = jnp.zeros((PATCH, channels), jnp.float32)
    spread[...] = jnp.zeros_like(spread)
    for i in range(PATCH):
        part = patch[i * PATCH : (i + 1) * PATCH]
        block = jnp.concatenate(
            [
                jnp.concatenate([part, blank], axis=1),
                jnp.concatenate([blank, part], axis=1),
            ],
            axis=0,
        ).astype(jnp.bfloat16)
        for n in range(group_cols // 2):
            spread[n, pl.ds(i * 128 + n * 2 * PATCH, 2 * PATCH), :] = block
    square = jnp.zeros((channels, channels), jnp.bfloat16)
    for layer in range(LAYERS):
        point = (point_ref[layer].astype(jnp.float32) * 0.5).astype(jnp.bfloat16)
        point_pair[layer, :channels, :channels] = point
        point_pair[layer, channels:, channels:] = point
        point_pair[layer, :channels, channels:] = square
        point_pair[layer, channels:, :channels] = square
    for layer in range(LAYERS):
        for dr in range(3):
            taps = depth_ref[layer, dr].astype(jnp.float32)
            for dc in range(3):
                depth_rows[(layer * 3 + dr) * 3 + dc] = jnp.broadcast_to(
                    taps[dc : dc + 1], (STRIP, channels)
                )

    for ref in (first, second):
        column = jnp.zeros(ref.shape[1:], jnp.float32)
        ref[0] = column
        ref[cols + 1] = column
        edge = jnp.zeros((cols + 2, EDGE, channels), jnp.float32)
        ref[:, :EDGE, :] = edge
        ref[:, EDGE + rows :, :] = edge

    row_block = 256
    row_cells = row_block // PATCH
    to_row = lax.broadcasted_iota(jnp.int32, (row_block, row_block), 0)
    from_row = lax.broadcasted_iota(jnp.int32, (row_block, row_block), 1)
    order = jnp.where(
        (from_row % PATCH == to_row // row_cells) & (from_row // PATCH == to_row % row_cells),
        1.0,
        0.0,
    ).astype(jnp.bfloat16)
    for b in range(height // row_block):
        ordered = jnp.dot(
            order,
            frame_ref[b * row_block : (b + 1) * row_block, :],
            preferred_element_type=jnp.float32,
        ).astype(jnp.bfloat16)
        for g in range(lane_groups):
            for i in range(PATCH):
                cells[
                    g, b * row_cells : (b + 1) * row_cells, i * 128 : (i + 1) * 128
                ] = ordered[i * row_cells : (i + 1) * row_cells, g * 128 : (g + 1) * 128]

    half_groups = max(lane_groups // 2, 1)

    def embed_step(step, carry):
        n = step // (lane_groups // half_groups)
        part = step % (lane_groups // half_groups)
        taken = cells[pl.ds(part * half_groups, half_groups)].reshape(
            half_groups * rows, PATCH * 128
        )
        half = jnp.dot(taken, spread[n], preferred_element_type=jnp.float32)
        for g in range(half_groups):
            value = gelu_of_half(half[g * rows : (g + 1) * rows])
            value = value.astype(jnp.bfloat16).astype(jnp.float32)
            column = (part * half_groups + g) * group_cols + 2 * n + 1
            first[column, EDGE : EDGE + rows, :] = value[:, :channels]
            first[column + 1, EDGE : EDGE + rows, :] = value[:, channels:]
        return carry

    lax.fori_loop(0, (group_cols // 2) * (lane_groups // half_groups), embed_step, 0)

    def layer_branch(layer, source, group):
        start = group * GROUP
        for p in range(GROUP // 2):
            for strip in range(rows // STRIP):
                sums = [None, None]
                for dr in range(3):
                    for cc in range(4):
                        taken = source[
                            start + 2 * p + cc, pl.ds(EDGE - 1 + strip * STRIP + dr, STRIP), :
                        ]
                        for o in range(2):
                            dc = cc - o
                            if 0 <= dc <= 2:
                                term = taken * depth_rows[layer * 9 + dr * 3 + dc]
                                sums[o] = term if sums[o] is None else sums[o] + term
                for o in range(2):
                    mixed[
                        p * rows + strip * STRIP : p * rows + (strip + 1) * STRIP,
                        o * channels : (o + 1) * channels,
                    ] = sums[o].astype(jnp.bfloat16)
        return jnp.dot(mixed[...], point_pair[layer], preferred_element_type=jnp.float32)

    def updated(source, group, half, p, o):
        column = group * GROUP + 2 * p + o + 1
        branch = gelu_of_half(
            half[p * rows : (p + 1) * rows, o * channels : (o + 1) * channels]
        )
        value = source[column, EDGE : EDGE + rows, :] + branch
        return column, value.astype(jnp.bfloat16).astype(jnp.float32)

    def layer_step(layer, source, target, group, carry):
        half = layer_branch(layer, source, group)
        for p in range(GROUP // 2):
            for o in range(2):
                column, value = updated(source, group, half, p, o)
                target[column, EDGE : EDGE + rows, :] = value
        return carry

    def last_step(source, group, total):
        half = layer_branch(LAYERS - 1, source, group)
        summed = jnp.zeros((rows, channels), jnp.float32)
        for p in range(GROUP // 2):
            for o in range(2):
                summed = summed + updated(source, group, half, p, o)[1]
        pooled = jnp.sum(summed.reshape(pool_rows, POOL, channels), axis=1) * (
            1.0 / (POOL * POOL)
        )
        own = lax.broadcasted_iota(jnp.int32, (pool_rows, channels), 0)
        features = jnp.concatenate(
            [jnp.where(own == r, pooled, 0.0) for r in range(pool_rows)], axis=1
        ).astype(jnp.bfloat16)
        observe_copy(group).wait()
        return total + jnp.dot(features, observe[group], preferred_element_type=jnp.float32)

    refs = (first, second)
    for layer in range(LAYERS - 1):
        lax.fori_loop(
            0,
            cols // GROUP,
            functools.partial(layer_step, layer, refs[layer % 2], refs[(layer + 1) % 2]),
            0,
        )
    total = lax.fori_loop(
        0,
        pool_cols,
        functools.partial(last_step, refs[(LAYERS - 1) % 2]),
        jnp.zeros((pool_rows, observe.shape[2]), jnp.float32),
    )
    out_ref[...] = jnp.sum(total, axis=0, keepdims=True)


def encode_whole(frame, patch_weight, depth_weight, point_weight, observe_weight):
    height, width = frame.shape
    channels = patch_weight.shape[1]
    rows, cols = height // PATCH, width // PATCH
    pool_cols, pool_rows, _, components = observe_weight.shape
    observe_weight = observe_weight.reshape(pool_cols, pool_rows * channels, components)
    vmem = pl.BlockSpec(memory_space=pltpu.VMEM)
    padded = (cols + 2, rows + 2 * EDGE, channels)
    return pl.pallas_call(
        encoder_kernel,
        out_shape=jax.ShapeDtypeStruct((1, components), jnp.float32),
        in_specs=[vmem, vmem, vmem, vmem, pl.BlockSpec(memory_space=pl.ANY)],
        out_specs=vmem,
        scratch_shapes=[
            pltpu.VMEM((width // 128, rows, PATCH * 128), jnp.bfloat16),
            pltpu.VMEM((128 // PATCH // 2, PATCH * 128, 2 * channels), jnp.bfloat16),
            pltpu.VMEM(padded, jnp.float32),
            pltpu.VMEM(padded, jnp.float32),
            pltpu.VMEM((GROUP // 2 * rows, 2 * channels), jnp.bfloat16),
            pltpu.VMEM((LAYERS * 9, STRIP, channels), jnp.float32),
            pltpu.VMEM((LAYERS, 2 * channels, 2 * channels), jnp.bfloat16),
            pltpu.VMEM(observe_weight.shape, jnp.bfloat16),
            pltpu.SemaphoreType.DMA((pool_cols,)),
        ],
        compiler_params=pltpu.CompilerParams(vmem_limit_bytes=60 * 1024 * 1024),
        name="encoder",
    )(frame, patch_weight, depth_weight, point_weight, observe_weight)


def complex_times(a, b):
    return (a[0] * b[0] - a[1] * b[1], a[0] * b[1] + a[1] * b[0])


def filter_kernel(
    count,
    observed_ref,
    map_ref,
    decay_ref,
    angle_ref,
    back_decay_ref,
    back_angle_ref,
    out_ref,
    gathered,
    send_sem,
    recv_sem,
):
    me = lax.axis_index("tm")
    barrier = pltpu.get_barrier_semaphore()

    def greet(step, carry):
        pl.semaphore_signal(
            barrier,
            inc=1,
            device_id={"tm": lax.rem(me + step, count)},
            device_id_type=pl.DeviceIdType.MESH,
        )
        return carry

    lax.fori_loop(1, count, greet, 0)

    mode_refs = (decay_ref, angle_ref, back_decay_ref, back_angle_ref)
    modes = decay_ref.shape[1]
    state = 2 * modes
    mode = lax.broadcasted_iota(jnp.int32, (modes, state), 0)
    component = lax.broadcasted_iota(jnp.int32, (modes, state), 1)
    repeat = jnp.where(component >> 1 == mode, 1.0, 0.0)
    doubled = jnp.dot(
        jnp.concatenate([ref[...] for ref in mode_refs], axis=0),
        repeat,
        precision=lax.Precision.HIGHEST,
        preferred_element_type=jnp.float32,
    )
    decay, angle, back_decay, back_angle = (doubled[k : k + 1] for k in range(4))
    drive = lax.dot_general(
        observed_ref[...],
        map_ref[...],
        (((1,), (1,)), ((), ())),
        precision=lax.Precision.HIGHEST,
        preferred_element_type=jnp.float32,
    ) * jnp.sqrt(1.0 - decay * decay)
    gathered[pl.ds(me, 1)] = drive.reshape(1, 1, state)
    pl.semaphore_wait(barrier, count - 1)

    def copy_to(step):
        return pltpu.make_async_remote_copy(
            src_ref=gathered.at[me],
            dst_ref=gathered.at[me],
            send_sem=send_sem.at[step],
            recv_sem=recv_sem.at[me],
            device_id={"tm": lax.rem(me + step, count)},
            device_id_type=pl.DeviceIdType.MESH,
        )

    def send(step, carry):
        copy_to(step).start()
        return carry

    lax.fori_loop(1, count, send, 0)

    forward = (decay * jnp.cos(angle), decay * jnp.sin(angle))
    backward = (back_decay * jnp.cos(back_angle), back_decay * jnp.sin(back_angle))
    both = complex_times(forward, backward)
    frame = lax.broadcasted_iota(jnp.int32, (count, state), 0)
    one = (jnp.ones((1, state), jnp.float32), jnp.zeros((1, state), jnp.float32))
    power, partial = one, one
    partial_sums = [one]
    for _ in range(count - 1):
        power = complex_times(power, both)
        partial = (partial[0] + power[0], partial[1] + power[1])
        partial_sums.append(partial)
    last = jnp.maximum(frame, me)
    sums = [jnp.zeros((count, state), jnp.float32) for _ in range(2)]
    for n in range(count):
        for k in range(2):
            sums[k] = jnp.where(last == count - 1 - n, partial_sums[n][k], sums[k])
    away = jnp.abs(frame - me)
    factor = tuple(jnp.where(frame > me, backward[k], forward[k]) for k in range(2))
    gain = tuple(sums)
    bit = 1
    while bit < count:
        taken = complex_times(gain, factor)
        chosen = (away & bit) != 0
        gain = tuple(jnp.where(chosen, taken[k], gain[k]) for k in range(2))
        factor = complex_times(factor, factor)
        bit = bit * 2
    weight = jnp.sqrt(1.0 - back_decay * back_decay)
    imaginary = (lax.broadcasted_iota(jnp.int32, (count, state), 1) & 1) == 1
    direct = gain[0] * weight
    crossed = jnp.where(imaginary, gain[1], -gain[1]) * weight

    def arrive(step, carry):
        source = lax.rem(me + step, count)
        pltpu.make_async_remote_copy(
            src_ref=gathered.at[source],
            dst_ref=gathered.at[source],
            send_sem=send_sem.at[step],
            recv_sem=recv_sem.at[source],
            device_id={"tm": source},
            device_id_type=pl.DeviceIdType.MESH,
        ).wait_recv()
        return carry

    lax.fori_loop(1, count, arrive, 0)
    drives = gathered[...].reshape(count, state)
    partner = jnp.where(
        imaginary, pltpu.roll(drives, 1, 1), pltpu.roll(drives, state - 1, 1)
    )
    out_ref[...] = jnp.sum(direct * drives + crossed * partner, axis=0, keepdims=True)

    def sent(step, carry):
        copy_to(step).wait_send()
        return carry

    lax.fori_loop(1, count, sent, 0)


def smoothed_state(observed, input_map, *modes):
    count = lax.axis_size("tm")
    state = input_map.shape[0]
    vmem = pl.BlockSpec(memory_space=pltpu.VMEM)
    return pl.pallas_call(
        functools.partial(filter_kernel, count),
        out_shape=jax.ShapeDtypeStruct((1, state), jnp.float32),
        in_specs=[vmem] * 6,
        out_specs=vmem,
        scratch_shapes=[
            pltpu.VMEM((count, 1, state), jnp.float32),
            pltpu.SemaphoreType.DMA((count,)),
            pltpu.SemaphoreType.DMA((count,)),
        ],
        compiler_params=pltpu.CompilerParams(collective_id=0, has_side_effects=True),
        name="filters",
    )(observed, input_map, *(mode.reshape(1, -1) for mode in modes))


def encode_tiles(frames, patch_weight, depth_weight, point_weight, observe_weight):
    frame_count, height, width = frames.shape
    grid_rows = height // PATCH
    grid_cols = width // PATCH
    channels = patch_weight.shape[1]
    hidden = embed(frames, patch_weight)
    for layer_index in range(LAYERS):
        widened = with_halo(hidden, (("tile", 2),), 1)
        padded = jnp.pad(widened, ((0, 0), (1, 1), (0, 0), (0, 0)))
        hidden = conv_layer(hidden, padded, depth_weight, point_weight, layer_index)
    pooled = jnp.mean(
        hidden.astype(jnp.float32).reshape(
            frame_count, grid_rows // POOL, POOL, grid_cols // POOL, POOL, channels
        ),
        axis=(2, 4),
    ).astype(jnp.bfloat16)
    features = pooled.transpose(0, 2, 1, 3).reshape(frame_count, -1)
    partial_value = jnp.dot(
        features,
        observe_weight.reshape(-1, observe_weight.shape[-1]),
        preferred_element_type=jnp.float32,
    )
    return lax.psum(partial_value, "tile")


def shards(
    movie_frames,
    patch_weight,
    depth_weight,
    point_weight,
    observe_weight,
    input_map,
    mode_decay,
    mode_angle,
    smooth_decay,
    smooth_angle,
    readout,
):
    tile_count = lax.axis_size("tile")
    encoder = (patch_weight, depth_weight, point_weight, observe_weight)
    if tile_count == 1:
        observed = encode_whole(movie_frames[0], *encoder)
    else:
        observed = encode_tiles(movie_frames, *encoder)
        share = readout.shape[0] // tile_count
        readout = lax.dynamic_slice_in_dim(readout, lax.axis_index("tile") * share, share, 0)
    smoothed = smoothed_state(
        observed, input_map, mode_decay, mode_angle, smooth_decay, smooth_angle
    )
    return jnp.dot(smoothed, readout.T, precision=lax.Precision.HIGHEST)


def solution(mesh):
    placed = (
        P("tm", None, "tile"),
        P(),
        P(),
        P(),
        P("tile", None, None, None),
        P(),
        P(),
        P(),
        P(),
        P(),
        P(),
    )
    return jax.shard_map(
        shards, mesh=mesh, in_specs=placed, out_specs=P("tm", "tile"), check_vma=False
    )
```
